512 devices in a mesh: wide: 64 (over y_hi, z, core), narrow: 8 (over y_lo, x).
Axes of the slice: x: 4, y: 8 (y_hi: 4, y_lo: 2; y = y_hi * 2 + y_lo), z: 8, core: 2. Of those that a mesh axis runs over, the one named last changes fastest.
Arguments:
- tokens: bfloat16 [262144, 768], P(('wide', 'narrow')), may hold values from -28 to 28
- proj_weight: bfloat16 [768, 2304], P('narrow'), may hold values from -0.375 to 0.375
- out_weight: bfloat16 [768, 768], P('narrow'), may hold values from -0.21875 to 0.21875
Outputs:
- mixed: bfloat16 [262144, 768], P(('wide', 'narrow'))
The draws below stay inside these ranges and needn't reach their ends.
All inputs are finite; a program needn't handle non-finite values.
Results may differ from the reference program's by a relative error of at most 0.012.
The reference program's roundings to bfloat16 on the way count: a program that leaves them out, or rounds other values in their place, can miss the bound.
Values may be sent and summed in bfloat16 or wider, within the bound.
A program may use at most 64 MiB of HBM per device.

```python
import jax
import jax.numpy as jnp
from jax import lax

MODEL_WIDTH = 768
HEAD_COUNT = 12
HEAD_WIDTH = 64
TOK_DEV = 512
SPACING_LEVEL1 = 4
SPACING_LEVEL2 = 16
SPACING_LEVEL3 = 256
TILE_TOKENS = 262144
N_NARROW = 8


def draw_tokens(key, part):
    key = jax.random.fold_in(key, 7)
    first_key = jax.random.fold_in(key, 0)
    values_out = jnp.clip(jax.random.normal(first_key, (TILE_TOKENS, MODEL_WIDTH), jnp.float32), -6.0, 6.0)
    return values_out.astype(jnp.bfloat16)


def levels(key, dims, cuts, smallest, top_value):
    def one(position, blocks):
        draws = jax.random.uniform(jax.random.fold_in(jax.random.fold_in(key, 6), position), (blocks,), jnp.float32, smallest / len(cuts), top_value / len(cuts))
        return jnp.repeat(jnp.exp(draws), dims[position] // blocks).reshape((-1,) + (1,) * (len(dims) - position - 1))

    level = one(*cuts[0])
    for cut in cuts[1:]:
        level = level * one(*cut)
    return level


def gaussian(key, shape, scale, limit, cuts=(), kind=jnp.bfloat16):
    values = scale * jax.random.normal(key, shape, jnp.float32)
    if cuts:
        values = values * levels(key, shape, cuts, -0.22, 0.18)
    return jnp.clip(values, -limit, limit).astype(kind)


def setup_inputs(seed: int = 0) -> dict:
    key_list = jax.random.split(jax.random.key(seed), 4)
    tokens = draw_tokens(jax.random.fold_in(key_list[3], 71), 0)
    proj_weight = gaussian(key_list[1], (MODEL_WIDTH, 3 * MODEL_WIDTH), (MODEL_WIDTH // 3) ** -0.5, 0.375, ((0, 8),))
    out_weight = gaussian(key_list[2], (MODEL_WIDTH, MODEL_WIDTH), MODEL_WIDTH ** -0.5, 0.21875, ((0, 8),))
    return dict(tokens=tokens, proj_weight=proj_weight, out_weight=out_weight)


score_scale = 0.125


def pick_rows(values_in, stride, start_index):
    count, heads_n, span_width = values_in.shape
    grouped = values_in.reshape(count // stride, stride, heads_n, span_width)
    chosen = jnp.arange(stride)[:, None] == start_index[None, :]
    return jnp.sum(jnp.where(chosen[None, :, :, None], grouped, jnp.zeros((), values_in.dtype)), axis=1).astype(values_in.dtype)


def scatter_rows(values_in, stride, start_index, background):
    count, heads_n, span_width = values_in.shape
    grouped = background.reshape(count, stride, heads_n, span_width)
    chosen = jnp.arange(stride)[:, None] == start_index[None, :]
    return jnp.where(chosen[None, :, :, None], values_in[:, None], grouped).reshape(background.shape)


def head_terms(operands):
    query_h, key_h, value_h = operands
    scores = jnp.einsum("sqe,ske->sqk", query_h.astype(jnp.float32), key_h.astype(jnp.float32)) * score_scale
    peak = jnp.max(scores, axis=-1, keepdims=True)
    weights = jnp.exp(scores - peak)
    totals = jnp.sum(weights, axis=-1, keepdims=True)
    probs = weights.astype(jnp.bfloat16).astype(jnp.float32)
    numerator = jnp.einsum("sqk,ske->sqe", probs, value_h.astype(jnp.float32))
    return peak, totals, numerator


def level_terms(queries, keys, values_in):
    outs_h = lax.map(head_terms, (jnp.moveaxis(queries, 2, 0), jnp.moveaxis(keys, 2, 0), jnp.moveaxis(values_in, 2, 0)))
    result = []
    for entry_value in outs_h:
        moved = jnp.moveaxis(entry_value, 0, 2)
        result.append(moved.reshape(moved.shape[0] * moved.shape[1], moved.shape[2], moved.shape[3]))
    return result


def combine(first, central_level, distant_level, head_index):
    start_index = head_index // SPACING_LEVEL1
    maximum_first, sum_first, weighted_first = first
    maximum_second = scatter_rows(central_level[0], SPACING_LEVEL2 // SPACING_LEVEL1, start_index, maximum_first)
    sum_second = scatter_rows(central_level[1], SPACING_LEVEL2 // SPACING_LEVEL1, start_index, jnp.zeros_like(sum_first))
    weighted_second = scatter_rows(central_level[2], SPACING_LEVEL2 // SPACING_LEVEL1, start_index, jnp.zeros_like(weighted_first))
    maximum_third = scatter_rows(distant_level[0], SPACING_LEVEL3 // SPACING_LEVEL1, start_index, maximum_first)
    sum_third = scatter_rows(distant_level[1], SPACING_LEVEL3 // SPACING_LEVEL1, start_index, jnp.zeros_like(sum_first))
    weighted_third = scatter_rows(distant_level[2], SPACING_LEVEL3 // SPACING_LEVEL1, start_index, jnp.zeros_like(weighted_first))
    highest = jnp.maximum(maximum_first, jnp.maximum(maximum_second, maximum_third))
    scale_one = jnp.exp(maximum_first - highest)
    scale_two = jnp.exp(maximum_second - highest)
    scale_three = jnp.exp(maximum_third - highest)
    totals = sum_first * scale_one + sum_second * scale_two + sum_third * scale_three
    numerator = weighted_first * scale_one + weighted_second * scale_two + weighted_third * scale_three
    return (numerator / totals).astype(jnp.bfloat16)


def reference(tokens, proj_weight, out_weight):
    query_matrix = jnp.dot(tokens, proj_weight[:, :MODEL_WIDTH], preferred_element_type=jnp.float32).astype(jnp.bfloat16).reshape(TILE_TOKENS, HEAD_COUNT, HEAD_WIDTH)
    key = jnp.dot(tokens, proj_weight[:, MODEL_WIDTH:2 * MODEL_WIDTH], preferred_element_type=jnp.float32).astype(jnp.bfloat16).reshape(TILE_TOKENS, HEAD_COUNT, HEAD_WIDTH)
    value_matrix = jnp.dot(tokens, proj_weight[:, 2 * MODEL_WIDTH:], preferred_element_type=jnp.float32).astype(jnp.bfloat16).reshape(TILE_TOKENS, HEAD_COUNT, HEAD_WIDTH)
    head_index = jnp.arange(HEAD_COUNT)
    query_first = pick_rows(query_matrix, SPACING_LEVEL1, head_index % SPACING_LEVEL1)
    key_first = pick_rows(key, SPACING_LEVEL1, head_index % SPACING_LEVEL1)
    value_first = pick_rows(value_matrix, SPACING_LEVEL1, head_index % SPACING_LEVEL1)
    segs_one = TILE_TOKENS // TOK_DEV
    first = level_terms(query_first.reshape(segs_one, -1, HEAD_COUNT, HEAD_WIDTH), key_first.reshape(segs_one, -1, HEAD_COUNT, HEAD_WIDTH), value_first.reshape(segs_one, -1, HEAD_COUNT, HEAD_WIDTH))
    second_pieces = TILE_TOKENS // (TOK_DEV * N_NARROW)
    central_pieces = [pick_rows(entry_value, SPACING_LEVEL2 // SPACING_LEVEL1, head_index // SPACING_LEVEL1).reshape(second_pieces, -1, HEAD_COUNT, HEAD_WIDTH) for entry_value in (query_first, key_first, value_first)]
    central_level = level_terms(central_pieces[0], central_pieces[1], central_pieces[2])
    distant_pieces = [pick_rows(entry_value, SPACING_LEVEL3 // SPACING_LEVEL1, head_index // SPACING_LEVEL1).reshape(1, -1, HEAD_COUNT, HEAD_WIDTH) for entry_value in (query_first, key_first, value_first)]
    distant_level = level_terms(distant_pieces[0], distant_pieces[1], distant_pieces[2])
    attended_first = combine(first, central_level, distant_level, head_index)
    attended_rows = scatter_rows(attended_first, SPACING_LEVEL1, head_index % SPACING_LEVEL1, jnp.zeros((TILE_TOKENS, HEAD_COUNT, HEAD_WIDTH), jnp.bfloat16)).reshape(TILE_TOKENS, MODEL_WIDTH)
    return jnp.dot(attended_rows, out_weight, preferred_element_type=jnp.float32).astype(jnp.bfloat16)
```

```python
import jax
import jax.numpy as jnp
from jax import lax
from jax.experimental import pallas as pl
from jax.experimental.pallas import tpu as pltpu
from jax.sharding import PartitionSpec as P

MESH = pl.DeviceIdType.MESH
BF = jnp.bfloat16
F32 = jnp.float32
SCALE = 0.125
LOW = -1e30


def iota(shape, dim):
    return lax.broadcasted_iota(jnp.int32, shape, dim)


def tile_of_row(r):
    j = r % 32
    s = jnp.where(j == 1, 16, jnp.where((j >= 2) & (j <= 16), j - 1, j))
    return 16 * s + 4 * ((r // 32) % 4) + r // 128


def dot(a, b):
    return jnp.dot(a, b, preferred_element_type=F32)


def dot_t(a, b):
    return lax.dot_general(a, b, (((1,), (1,)), ((), ())), preferred_element_type=F32)


def soft(q, k, v, mask=None):
    s = dot_t(q, k) * SCALE
    if mask is not None:
        s = jnp.where(mask, s, LOW)
    peak = jnp.max(s, axis=-1, keepdims=True)
    w = jnp.exp(s - peak)
    return peak, jnp.sum(w, axis=-1, keepdims=True), dot(w.astype(BF), v)


def merge(a, b):
    top = jnp.maximum(a[0], b[0])
    ea, eb = jnp.exp(a[0] - top), jnp.exp(b[0] - top)
    return top, a[1] * ea + b[1] * eb, a[2] * ea + b[2] * eb


def kernel(
    tok_hbm, wp_hbm, wo_hbm, out_ref,
    tok, perm, back, xp, wp, wo, qkv, kv2, kv3, q3, part_out, part_in, att, y,
    loc_sem, ws, wr, os_, or_, s2, r2, s3, r3,
):
    w, n = lax.axis_index("wide"), lax.axis_index("narrow")
    x, yl, core, z, yh = n % 4, n // 4, w % 2, (w // 2) % 8, w // 16
    yy = 2 * yh + yl

    def dev(dx=0, dy=0, dz=0, dc=0):
        y_ = (yy + dy) % 8
        return ((y_ // 2) * 16 + ((z + dz) % 8) * 2 + (core + dc) % 2, (y_ % 2) * 4 + (x + dx) % 4)

    def narrow_dev(k):
        return (w, (n + k) % 8)

    barrier = pltpu.get_barrier_semaphore()
    partners = (
        [dev(dx=k) for k in (1, 2, 3)] + [dev(dy=k) for k in range(1, 8)] + [dev(dz=k) for k in range(1, 8)] + [dev(dc=1)]
    )
    diag = [(w, (1 - yl) * 4 + (x + k) % 4) for k in (1, 2, 3)]
    partners = partners + diag
    for p in partners:
        pl.semaphore_signal(barrier, inc=1, device_id=p, device_id_type=MESH)

    def send(src, dst, ss, rs, to):
        c = pltpu.make_async_remote_copy(
            src_ref=src, dst_ref=dst, send_sem=ss, recv_sem=rs, device_id=to, device_id_type=MESH
        )
        c.start()
        return c

    mine = pl.ds(pl.multiple_of(96 * n, 32), 96)
    loc = [
        pltpu.make_async_copy(tok_hbm, tok, loc_sem.at[0]),
        pltpu.make_async_copy(wp_hbm, wp.at[mine], loc_sem.at[1]),
        pltpu.make_async_copy(wo_hbm, wo.at[mine], loc_sem.at[2]),
    ]
    for c in loc:
        c.start()
    pl.semaphore_wait(barrier, len(partners))

    class Gather:
        def __init__(self, src, buf, cuts, ss, rs):
            self.src, self.buf, self.ss, self.rs = src, buf, ss, rs
            q = [pl.ds(a, b - a) for a, b in zip(cuts, cuts[1:])]
            self.q = q
            self.left, self.right, self.full = pl.ds(0, cuts[2]), pl.ds(cuts[2], cuts[4] - cuts[2]), pl.ds(0, cuts[4])
            self.sent, self.passed = [], []
            self.k = 0

        def at(self, dx, other, cols):
            half = (1 - yl) if other else yl
            j = half * 4 + (x + dx) % 4
            return self.buf.at[pl.ds(pl.multiple_of(96 * j + 48 * core, 16), 48), cols]

        def go(self, src, dst, to):
            c = send(src, dst, self.ss.at[self.k], self.rs.at[self.k], to)
            self.k += 1
            self.sent.append(c)
            return c

        def twin(self, *refs):
            for ref in refs:
                self.passed.append(self.go(ref, ref, dev(dc=1)))

        def relay(self, wait, ref):
            wait.wait_recv()
            self.twin(ref)

        def phase_a(self):
            def own(cols, to):
                src = self.src.at[pl.ds(pl.multiple_of(48 * core, 16), 48), cols]
                return self.go(src, self.at(0, False, cols), to)

            self.a = [
                own(self.full, dev(dx=1)), own(self.full, dev(dx=3)), own(self.left, dev(dy=1)), own(self.right, dev(dy=7))
            ]

        def phase_b(self):
            a = self.a
            a[0].wait_recv()
            b1 = self.go(self.at(3, False, self.left), self.at(3, False, self.left), dev(dx=1))
            b3 = self.go(self.at(3, False, self.full), self.at(3, False, self.full), dev(dy=1))
            a[1].wait_recv()
            b2 = self.go(self.at(1, False, self.right), self.at(1, False, self.right), dev(dx=3))
            b4 = self.go(self.at(1, False, self.full), self.at(1, False, self.full), dev(dy=7))
            self.b = [b1, b2, b3, b4]
            self.twin(self.at(3, False, self.full), self.at(1, False, self.full))
            self.relay(a[2], self.at(0, True, self.left))
            self.relay(a[3], self.at(0, True, self.right))

        def phase_c(self):
            b1, b2, b3, b4 = self.b
            q = self.q
            b1.wait_recv()
            c3 = self.go(self.at(2, False, q[0]), self.at(2, False, q[0]), dev(dy=1))
            b2.wait_recv()
            c4 = self.go(self.at(2, False, q[3]), self.at(2, False, q[3]), dev(dy=7))
            b3.wait_recv()
            c1 = self.go(self.at(3, True, q[1]), self.at(3, True, q[1]), dev(dx=1))
            b4.wait_recv()
            c2 = self.go(self.at(1, True, q[2]), self.at(1, True, q[2]), dev(dx=3))
            self.c = [c1, c2, c3, c4]
            self.twin(self.at(2, False, self.full), self.at(3, True, self.full), self.at(1, True, self.full))

        def finish(self):
            for c, k in zip(self.c, (1, 2, 0, 3)):
                self.relay(c, self.at(2, True, self.q[k]))
            for c in self.passed:
                c.wait_recv()
            for c in self.sent:
                c.wait_send()

    proj = Gather(wp_hbm, wp, (0, 512, 1152, 1792, 2304), ws, wr)
    outp = Gather(wo_hbm, wo, (0, 256, 384, 512, 768), os_, or_)
    proj.phase_a()

    perm[...] = jnp.where(iota((512, 512), 1) == tile_of_row(iota((512, 512), 0)), 1.0, 0.0).astype(BF)
    back[...] = jnp.where(iota((512, 512), 0) == tile_of_row(iota((512, 512), 1)), 1.0, 0.0).astype(BF)
    proj.phase_b()
    loc[0].wait()
    xp[...] = dot(perm[...], tok[...]).astype(BF)
    proj.phase_c()
    outp.phase_a()
    loc[1].wait()
    proj.finish()

    for cp in range(2):
        cols = [768 * m + 128 * (2 * t + cp) for m in range(3) for t in range(3)]
        wc = jnp.concatenate([wp[:, c : c + 128] for c in cols], axis=1)
        qkv[256 * cp : 256 * cp + 256, :] = dot(xp[256 * cp : 256 * cp + 256, :], wc).astype(BF)

    low = iota((1, 128), 1) < 64
    row16 = iota((16, 128), 0)

    def second(m, cp, t):
        a = 256 * cp + 32 * t
        c = 384 * m + 128 * t
        return jnp.where(low, qkv[a : a + 32, c : c + 128].astype(F32), qkv[a + 128 : a + 160, c : c + 128].astype(F32))

    zeros8 = jnp.zeros((8, 128), F32)
    third = [jnp.zeros((16, 128), F32) for _ in range(3)]
    for m in range(3):
        for cp in range(2):
            for t in range(3):
                v = second(m, cp, t)
                i = 2 * t + cp
                if m > 0:
                    kv2[m - 1, pl.ds(pl.multiple_of(32 * n, 32), 32), 128 * i : 128 * i + 128] = v.astype(BF)
                e = jnp.concatenate([v[:8], zeros8], axis=0)
                if i:
                    e = pltpu.roll(e, 2 * i, 0)
                third[m] = jnp.where((row16 >= 2 * i) & (row16 < 2 * i + 2), e, third[m])
    q3[z] = third[0].astype(BF)
    for m in range(2):
        kv3[m, core, x, yy] = third[m + 1].astype(BF)

    sent = []
    k3 = 0

    def go3(src, dst, to):
        nonlocal k3
        c = send(src, dst, s3.at[k3], r3.at[k3], to)
        k3 += 1
        sent.append(c)
        return c

    own3 = kv3.at[:, core, x, yy]
    a3 = [go3(own3, own3, dev(dy=k)) for k in range(1, 8)]
    sq = [go3(q3.at[z], q3.at[z], dev(dz=k)) for k in range(1, 8)]
    own2 = kv2.at[:, pl.ds(pl.multiple_of(32 * n, 32), 32)]
    to2 = [dev(dx=1), dev(dx=3), dev(dx=2), (w, (1 - yl) * 4 + x)] + diag
    g2 = [send(own2, own2, s2.at[k], r2.at[k], p) for k, p in enumerate(to2)]
    sent += g2

    first = {}

    def level1(cp, t):
        for lo in range(2):
            r = slice(256 * cp + 128 * lo, 256 * cp + 128 * lo + 128)
            lanes = low if lo == 0 else ~low
            q = jnp.where(lanes, qkv[r, 128 * t : 128 * t + 128].astype(F32), 0.0).astype(BF)
            pk, tot, num = soft(q, qkv[r, 384 + 128 * t : 512 + 128 * t], qkv[r, 768 + 128 * t : 896 + 128 * t])
            att[r, 128 * t : 128 * t + 128] = jnp.where(lanes, num / tot, 0.0).astype(BF)
            b = slice(32 * t, 32 * t + 32)
            first[cp, t, lo] = pk[b], tot[b], num[b]

    for t in range(3):
        level1(0, t)
    for c in a3:
        c.wait_recv()
    plane = kv3.at[:, core, x]
    b3 = [go3(plane, plane, dev(dx=k)) for k in (1, 3, 2)]
    for t in range(3):
        level1(1, t)
    outp.phase_b()
    for c in b3:
        c.wait_recv()
    half = kv3.at[:, core]
    c3 = go3(half, half, dev(dc=1))
    outp.phase_c()
    for c in sq:
        c.wait_recv()
    c3.wait_recv()

    qa = q3[...].reshape(128, 128).astype(F32)
    qs = jnp.concatenate([jnp.where(low, qa, 0.0), jnp.where(low, 0.0, qa)], axis=0).astype(BF)
    same = (iota((256, 1024), 0) % 16) // 2 == (iota((256, 1024), 1) % 16) // 2
    pk, tot, num = soft(qs, kv3[0].reshape(1024, 128), kv3[1].reshape(1024, 128), same)
    num = jnp.where(low, num[:128], num[128:]).reshape(8, 16, 128)
    row, lane = iota((8, 16, 128), 1), iota((8, 16, 128), 2)

    def to_lanes(v):
        a, b = v[:128].reshape(8, 16, 1), v[128:].reshape(8, 16, 1)
        u = jnp.where(lane == row, a, jnp.where(lane == row + 64, b, 0.0))
        return jnp.sum(u, axis=1, keepdims=True)

    part_out[...] = jnp.where(row < 12, num, jnp.where(row == 12, to_lanes(pk), to_lanes(tot)))
    sp = [go3(part_out.at[(z + k) % 8], part_in.at[z], dev(dz=k)) for k in range(1, 8)]
    part_in[z] = part_out[z]

    for c in g2:
        c.wait_recv()
    both = {}
    for cp in range(2):
        for t in range(3):
            i = 2 * t + cp
            v = second(0, cp, t)
            q = jnp.concatenate([jnp.where(low, v, 0.0), jnp.where(low, 0.0, v)], axis=0).astype(BF)
            pk, tot, num = soft(q, kv2[0, :, 128 * i : 128 * i + 128], kv2[1, :, 128 * i : 128 * i + 128])
            for lo in range(2):
                b = slice(32 * lo, 32 * lo + 32)
                both[cp, t, lo] = merge(first[cp, t, lo], (pk[b], tot[b], num[b]))

    outp.finish()
    loc[2].wait()
    for c in sp:
        c.wait_recv()
    p = part_in[...]

    def from_lanes(v):
        a = jnp.sum(jnp.where(lane == row, v, 0.0), axis=-1, keepdims=True)
        b = jnp.sum(jnp.where(lane == row + 64, v, 0.0), axis=-1, keepdims=True)
        return jnp.where(lane < 64, a, b)

    pk, tot = from_lanes(p[:, 12:13]), from_lanes(p[:, 13:14])
    top = jnp.max(pk, axis=0)
    e = jnp.exp(pk - top[None])
    dist = (top, jnp.sum(tot * e, axis=0), jnp.sum(p * e, axis=0))

    use = iota((8, 128), 0) < 2
    for cp in range(2):
        for t in range(3):
            i = 2 * t + cp
            d = [pltpu.roll(v, 16 - 2 * i, 0)[:8] if i else v[:8] for v in dist]
            d = (jnp.where(use, d[0], LOW), jnp.where(use, d[1], 0.0), jnp.where(use, d[2], 0.0))
            for lo in range(2):
                lanes = low if lo == 0 else ~low
                pk, tot, num = both[cp, t, lo]
                _, tot8, num8 = merge((pk[:8], tot[:8], num[:8]), d)
                o = jnp.concatenate([num8 / tot8, num[8:] / tot[8:]], axis=0)
                a = 256 * cp + 128 * lo + 32 * t
                att[a : a + 32, 128 * t : 128 * t + 128] = jnp.where(lanes, o, 0.0).astype(BF)
        wc = jnp.concatenate([wo[128 * (2 * t + cp) : 128 * (2 * t + cp) + 128, :] for t in range(3)], axis=0)
        y[256 * cp : 256 * cp + 256, :] = dot(att[256 * cp : 256 * cp + 256, :], wc).astype(BF)
    out_ref[...] = dot(back[...], y[...]).astype(BF)
    for c in sent:
        c.wait_send()


def shards(tokens, proj_weight, out_weight):
    hbm = pl.BlockSpec(memory_space=pl.ANY)
    dma = pltpu.SemaphoreType.DMA
    return pl.pallas_call(
        kernel,
        out_shape=jax.ShapeDtypeStruct((512, 768), BF),
        in_specs=[hbm] * 3,
        out_specs=pl.BlockSpec(memory_space=pltpu.VMEM),
        scratch_shapes=[
            pltpu.VMEM((512, 768), BF),
            pltpu.VMEM((512, 512), BF),
            pltpu.VMEM((512, 512), BF),
            pltpu.VMEM((512, 768), BF),
            pltpu.VMEM((768, 2304), BF),
            pltpu.VMEM((768, 768), BF),
            pltpu.VMEM((512, 1152), BF),
            pltpu.VMEM((2, 256, 768), BF),
            pltpu.VMEM((2, 2, 4, 8, 16, 128), BF),
            pltpu.VMEM((8, 16, 128), BF),
            pltpu.VMEM((8, 16, 128), F32),
            pltpu.VMEM((8, 16, 128), F32),
            pltpu.VMEM((512, 384), BF),
            pltpu.VMEM((512, 768), BF),
            dma((3,)),
            dma((24,)), dma((24,)), dma((24,)), dma((24,)),
            dma((8,)), dma((8,)), dma((32,)), dma((32,)),
        ],
        compiler_params=pltpu.CompilerParams(collective_id=0, has_side_effects=True, vmem_limit_bytes=56 << 20),
    )(tokens, proj_weight, out_weight)


def solution(mesh):
    return jax.shard_map(
        shards,
        mesh=mesh,
        in_specs=(P(("wide", "narrow"), None), P("narrow", None), P("narrow", None)),
        out_specs=P(("wide", "narrow"), None),
        check_vma=False,
    )
```

```python
import jax
import jax.numpy as jnp
from jax import lax
from jax.experimental import pallas as pl
from jax.experimental.pallas import tpu as pltpu
from jax.sharding import PartitionSpec as P

MESH = pl.DeviceIdType.MESH
BF = jnp.bfloat16
F32 = jnp.float32
SCALE = 0.125
LOW = -1e30


def iota(shape, dim):
    return lax.broadcasted_iota(jnp.int32, shape, dim)


def tile_of_row(r):
    j = r % 32
    s = jnp.where(j == 1, 16, jnp.where((j >= 2) & (j <= 16), j - 1, j))
    return 16 * s + 4 * ((r // 32) % 4) + r // 128


def dot(a, b):
    return jnp.dot(a, b, preferred_element_type=F32)


def dot_t(a, b):
    return lax.dot_general(a, b, (((1,), (1,)), ((), ())), preferred_element_type=F32)


def soft(q, k, v, mask=None):
    s = dot_t(q, k) * SCALE
    if mask is not None:
        s = jnp.where(mask, s, LOW)
    peak = jnp.max(s, axis=-1, keepdims=True)
    w = jnp.exp(s - peak)
    return peak, jnp.sum(w, axis=-1, keepdims=True), dot(w.astype(BF), v)


def merge(a, b):
    top = jnp.maximum(a[0], b[0])
    ea, eb = jnp.exp(a[0] - top), jnp.exp(b[0] - top)
    return top, a[1] * ea + b[1] * eb, a[2] * ea + b[2] * eb


def kernel(
    tok_hbm, wp_hbm, wo_hbm, out_ref,
    tok, perm, back, xp, wp, wo, qkv, kv2, kv3, q3, part_out, part_in, att, y,
    loc_sem, ws, wr, s2, r2, s3, r3,
):
    w, n = lax.axis_index("wide"), lax.axis_index("narrow")
    x, yl, core, z, yh = n % 4, n // 4, w % 2, (w // 2) % 8, w // 16
    yy = 2 * yh + yl

    def dev(dx=0, dy=0, dz=0, dc=0):
        y_ = (yy + dy) % 8
        return ((y_ // 2) * 16 + ((z + dz) % 8) * 2 + (core + dc) % 2, (y_ % 2) * 4 + (x + dx) % 4)

    barrier = pltpu.get_barrier_semaphore()
    partners = (
        [dev(dx=k) for k in (1, 2, 3)] + [dev(dy=k) for k in range(1, 8)] + [dev(dz=k) for k in range(1, 8)] + [dev(dc=1)]
    )
    diag = [(w, (1 - yl) * 4 + (x + k) % 4) for k in (1, 2, 3)]
    partners = partners + diag
    for p in partners:
        pl.semaphore_signal(barrier, inc=1, device_id=p, device_id_type=MESH)

    def send(src, dst, ss, rs, to):
        c = pltpu.make_async_remote_copy(
            src_ref=src, dst_ref=dst, send_sem=ss, recv_sem=rs, device_id=to, device_id_type=MESH
        )
        c.start()
        return c

    mine = pl.ds(pl.multiple_of(96 * n, 32), 96)
    loc = [
        pltpu.make_async_copy(tok_hbm, tok, loc_sem.at[0]),
        pltpu.make_async_copy(wp_hbm, wp.at[mine], loc_sem.at[1]),
        pltpu.make_async_copy(wo_hbm, wo.at[mine], loc_sem.at[2]),
    ]
    for c in loc:
        c.start()
    pl.semaphore_wait(barrier, len(partners))

    class Gather:
        def __init__(self, src, buf, base, cuts, ss, rs):
            self.src, self.buf, self.ss, self.rs = src, buf, ss, rs
            cuts = [base + c for c in cuts]
            q = [pl.ds(a, b - a) for a, b in zip(cuts, cuts[1:])]
            self.q = q
            self.left, self.right = pl.ds(cuts[0], cuts[2] - cuts[0]), pl.ds(cuts[2], cuts[4] - cuts[2])
            self.full = pl.ds(cuts[0], cuts[4] - cuts[0])
            self.sent, self.passed = [], []
            self.k = 0

        def at(self, dx, other, cols):
            half = (1 - yl) if other else yl
            j = half * 4 + (x + dx) % 4
            return self.buf.at[pl.ds(pl.multiple_of(96 * j + 48 * core, 16), 48), cols]

        def go(self, src, dst, to):
            c = send(src, dst, self.ss.at[self.k], self.rs.at[self.k], to)
            self.k += 1
            self.sent.append(c)
            return c

        def twin(self, *refs):
            for ref in refs:
                self.passed.append(self.go(ref, ref, dev(dc=1)))

        def relay(self, wait, ref):
            wait.wait_recv()
            self.twin(ref)

        def phase_a(self):
            def own(cols, to):
                src = self.src.at[pl.ds(pl.multiple_of(48 * core, 16), 48), cols]
                return self.go(src, self.at(0, False, cols), to)

            self.a = [
                own(self.full, dev(dx=1)), own(self.full, dev(dx=3)), own(self.left, dev(dy=1)), own(self.right, dev(dy=7))
            ]

        def phase_b(self):
            a = self.a
            a[0].wait_recv()
            b1 = self.go(self.at(3, False, self.left), self.at(3, False, self.left), dev(dx=1))
            b3 = self.go(self.at(3, False, self.full), self.at(3, False, self.full), dev(dy=1))
            a[1].wait_recv()
            b2 = self.go(self.at(1, False, self.right), self.at(1, False, self.right), dev(dx=3))
            b4 = self.go(self.at(1, False, self.full), self.at(1, False, self.full), dev(dy=7))
            self.b = [b1, b2, b3, b4]
            self.twin(self.at(3, False, self.full), self.at(1, False, self.full))
            self.relay(a[2], self.at(0, True, self.left))
            self.relay(a[3], self.at(0, True, self.right))

        def phase_c(self):
            b1, b2, b3, b4 = self.b
            q = self.q
            b1.wait_recv()
            c3 = self.go(self.at(2, False, q[0]), self.at(2, False, q[0]), dev(dy=1))
            b2.wait_recv()
            c4 = self.go(self.at(2, False, q[3]), self.at(2, False, q[3]), dev(dy=7))
            b3.wait_recv()
            c1 = self.go(self.at(3, True, q[1]), self.at(3, True, q[1]), dev(dx=1))
            b4.wait_recv()
            c2 = self.go(self.at(1, True, q[2]), self.at(1, True, q[2]), dev(dx=3))
            self.c = [c1, c2, c3, c4]
            self.twin(self.at(2, False, self.full), self.at(3, True, self.full), self.at(1, True, self.full))

        def finish(self):
            for c, k in zip(self.c, (1, 2, 0, 3)):
                self.relay(c, self.at(2, True, self.q[k]))
            for c in self.passed:
                c.wait_recv()
            for c in self.sent:
                c.wait_send()

    def group(src, buf, base, k):
        return Gather(src, buf, base, (0, 128, 384, 512, 768), ws.at[k], wr.at[k])

    gq, gk, gv = (group(wp_hbm, wp, 768 * k, k) for k in range(3))
    outp = group(wo_hbm, wo, 0, 3)
    gk.phase_a()
    gv.phase_a()

    perm[...] = jnp.where(iota((512, 512), 1) == tile_of_row(iota((512, 512), 0)), 1.0, 0.0).astype(BF)
    gk.phase_b()
    gq.phase_a()
    loc[0].wait()
    xp[...] = dot(perm[...], tok[...]).astype(BF)
    gv.phase_b()
    gk.phase_c()
    back[...] = jnp.where(iota((512, 512), 0) == tile_of_row(iota((512, 512), 1)), 1.0, 0.0).astype(BF)
    gq.phase_b()
    gv.phase_c()
    loc[1].wait()

    def project(m):
        for cp in range(2):
            wc = jnp.concatenate([wp[:, c : c + 128] for c in (768 * m + 128 * (2 * t + cp) for t in range(3))], axis=1)
            r = slice(256 * cp, 256 * cp + 256)
            qkv[r, 384 * m : 384 * m + 384] = dot(xp[r, :], wc).astype(BF)

    low = iota((1, 128), 1) < 64
    row16 = iota((16, 128), 0)
    zeros8 = jnp.zeros((8, 128), F32)

    def second(m, cp, t):
        a = 256 * cp + 32 * t
        c = 384 * m + 128 * t
        return jnp.where(low, qkv[a : a + 32, c : c + 128].astype(F32), qkv[a + 128 : a + 160, c : c + 128].astype(F32))

    def third(m):
        out = jnp.zeros((16, 128), F32)
        for cp in range(2):
            for t in range(3):
                v = second(m, cp, t)
                i = 2 * t + cp
                if m > 0:
                    kv2[m - 1, pl.ds(pl.multiple_of(32 * n, 32), 32), 128 * i : 128 * i + 128] = v.astype(BF)
                e = jnp.concatenate([v[:8], zeros8], axis=0)
                if i:
                    e = pltpu.roll(e, 2 * i, 0)
                out = jnp.where((row16 >= 2 * i) & (row16 < 2 * i + 2), e, out)
        if m > 0:
            kv3[m - 1, core, x, yy] = out.astype(BF)
        else:
            q3[z] = out.astype(BF)

    gk.finish()
    project(1)
    third(1)
    gq.phase_c()
    gv.finish()
    project(2)
    third(2)

    sent = []
    k2 = k3 = 0

    def go3(src, dst, to):
        nonlocal k3
        c = send(src, dst, s3.at[k3], r3.at[k3], to)
        k3 += 1
        sent.append(c)
        return c

    def go2(ref, to):
        nonlocal k2
        c = send(ref, ref, s2.at[k2], r2.at[k2], to)
        k2 += 1
        sent.append(c)
        return c

    full2, left2, right2 = pl.ds(0, 768), pl.ds(0, 384), pl.ds(384, 384)

    def at2(dx, other, cols=full2):
        j = ((1 - yl) if other else yl) * 4 + (x + dx) % 4
        return kv2.at[:, pl.ds(pl.multiple_of(32 * j, 32), 32), cols]

    own3 = kv3.at[:, core, x, yy]
    a3 = [go3(own3, own3, dev(dy=k)) for k in (4, 3, 5, 2, 6, 1, 7)]
    pair = (w, (1 - yl) * 4 + x)
    u = [go2(at2(0, False), to) for to in (dev(dx=1), dev(dx=3), pair)]
    outp.phase_a()

    gq.finish()
    project(0)
    third(0)
    sq = [go3(q3.at[z], q3.at[z], dev(dz=k)) for k in (4, 3, 5, 2, 6, 1, 7)]

    first = {}

    def level1(cp, t):
        for lo in range(2):
            r = slice(256 * cp + 128 * lo, 256 * cp + 128 * lo + 128)
            lanes = low if lo == 0 else ~low
            q = jnp.where(lanes, qkv[r, 128 * t : 128 * t + 128].astype(F32), 0.0).astype(BF)
            pk, tot, num = soft(q, qkv[r, 384 + 128 * t : 512 + 128 * t], qkv[r, 768 + 128 * t : 896 + 128 * t])
            att[r, 128 * t : 128 * t + 128] = jnp.where(lanes, num / tot, 0.0).astype(BF)
            b = slice(32 * t, 32 * t + 32)
            first[cp, t, lo] = pk[b], tot[b], num[b]

    level1(0, 0)
    for c in a3:
        c.wait_recv()
    plane = kv3.at[:, core, x]
    b3 = [go3(plane, plane, dev(dx=k)) for k in (2, 1, 3)]
    u[0].wait_recv()
    v1 = go2(at2(3, False, left2), dev(dx=1))
    u[1].wait_recv()
    v2 = go2(at2(1, False, right2), dev(dx=3))
    u[2].wait_recv()
    g2 = [go2(at2(0, True), dev(dx=1)), go2(at2(0, True), dev(dx=3))]
    level1(0, 1)
    level1(0, 2)
    outp.phase_b()
    level1(1, 0)
    v1.wait_recv()
    v2.wait_recv()
    g2.append(go2(at2(2, False), pair))
    level1(1, 1)
    level1(1, 2)
    for c in b3:
        c.wait_recv()
    half = kv3.at[:, core]
    c3 = go3(half, half, dev(dc=1))
    outp.phase_c()
    for c in sq:
        c.wait_recv()
    c3.wait_recv()

    qa = q3[...].reshape(128, 128).astype(F32)
    qs = jnp.concatenate([jnp.where(low, qa, 0.0), jnp.where(low, 0.0, qa)], axis=0).astype(BF)
    same = (iota((256, 1024), 0) % 16) // 2 == (iota((256, 1024), 1) % 16) // 2
    pk, tot, num = soft(qs, kv3[0].reshape(1024, 128), kv3[1].reshape(1024, 128), same)
    num = jnp.where(low, num[:128], num[128:]).reshape(8, 16, 128)
    row, lane = iota((8, 16, 128), 1), iota((8, 16, 128), 2)

    def to_lanes(v):
        a, b = v[:128].reshape(8, 16, 1), v[128:].reshape(8, 16, 1)
        u = jnp.where(lane == row, a, jnp.where(lane == row + 64, b, 0.0))
        return jnp.sum(u, axis=1, keepdims=True)

    part_out[...] = jnp.where(row < 12, num, jnp.where(row == 12, to_lanes(pk), to_lanes(tot)))
    sp = [go3(part_out.at[(z + k) % 8], part_in.at[z], dev(dz=k)) for k in (4, 3, 5, 2, 6, 1, 7)]
    part_in[z] = part_out[z]

    for c in g2:
        c.wait_recv()
    both = {}
    for cp in range(2):
        for t in range(3):
            i = 2 * t + cp
            v = second(0, cp, t)
            q = jnp.concatenate([jnp.where(low, v, 0.0), jnp.where(low, 0.0, v)], axis=0).astype(BF)
            pk, tot, num = soft(q, kv2[0, :, 128 * i : 128 * i + 128], kv2[1, :, 128 * i : 128 * i + 128])
            for lo in range(2):
                b = slice(32 * lo, 32 * lo + 32)
                both[cp, t, lo] = merge(first[cp, t, lo], (pk[b], tot[b], num[b]))

    outp.finish()
    loc[2].wait()
    for c in sp:
        c.wait_recv()
    p = part_in[...]

    def from_lanes(v):
        a = jnp.sum(jnp.where(lane == row, v, 0.0), axis=-1, keepdims=True)
        b = jnp.sum(jnp.where(lane == row + 64, v, 0.0), axis=-1, keepdims=True)
        return jnp.where(lane < 64, a, b)

    pk, tot = from_lanes(p[:, 12:13]), from_lanes(p[:, 13:14])
    top = jnp.max(pk, axis=0)
    e = jnp.exp(pk - top[None])
    dist = (top, jnp.sum(tot * e, axis=0), jnp.sum(p * e, axis=0))

    use = iota((8, 128), 0) < 2
    for cp in range(2):
        for t in range(3):
            i = 2 * t + cp
            d = [pltpu.roll(v, 16 - 2 * i, 0)[:8] if i else v[:8] for v in dist]
            d = (jnp.where(use, d[0], LOW), jnp.where(use, d[1], 0.0), jnp.where(use, d[2], 0.0))
            for lo in range(2):
                lanes = low if lo == 0 else ~low
                pk, tot, num = both[cp, t, lo]
                _, tot8, num8 = merge((pk[:8], tot[:8], num[:8]), d)
                o = jnp.concatenate([num8 / tot8, num[8:] / tot[8:]], axis=0)
                a = 256 * cp + 128 * lo + 32 * t
                att[a : a + 32, 128 * t : 128 * t + 128] = jnp.where(lanes, o, 0.0).astype(BF)
        wc = jnp.concatenate([wo[128 * (2 * t + cp) : 128 * (2 * t + cp) + 128, :] for t in range(3)], axis=0)
        y[256 * cp : 256 * cp + 256, :] = dot(att[256 * cp : 256 * cp + 256, :], wc).astype(BF)
    out_ref[...] = dot(back[...], y[...]).astype(BF)
    for c in sent:
        c.wait_send()


def shards(tokens, proj_weight, out_weight):
    hbm = pl.BlockSpec(memory_space=pl.ANY)
    dma = pltpu.SemaphoreType.DMA
    return pl.pallas_call(
        kernel,
        out_shape=jax.ShapeDtypeStruct((512, 768), BF),
        in_specs=[hbm] * 3,
        out_specs=pl.BlockSpec(memory_space=pltpu.VMEM),
        scratch_shapes=[
            pltpu.VMEM((512, 768), BF),
            pltpu.VMEM((512, 512), BF),
            pltpu.VMEM((512, 512), BF),
            pltpu.VMEM((512, 768), BF),
            pltpu.VMEM((768, 2304), BF),
            pltpu.VMEM((768, 768), BF),
            pltpu.VMEM((512, 1152), BF),
            pltpu.VMEM((2, 256, 768), BF),
            pltpu.VMEM((2, 2, 4, 8, 16, 128), BF),
            pltpu.VMEM((8, 16, 128), BF),
            pltpu.VMEM((8, 16, 128), F32),
            pltpu.VMEM((8, 16, 128), F32),
            pltpu.VMEM((512, 384), BF),
            pltpu.VMEM((512, 768), BF),
            dma((3,)),
            dma((4, 23)), dma((4, 23)), dma((8,)), dma((8,)), dma((25,)), dma((25,)),
        ],
        compiler_params=pltpu.CompilerParams(collective_id=0, has_side_effects=True, vmem_limit_bytes=56 << 20),
    )(tokens, proj_weight, out_weight)


def solution(mesh):
    return jax.shard_map(
        shards,
        mesh=mesh,
        in_specs=(P(("wide", "narrow"), None), P("narrow", None), P("narrow", None)),
        out_specs=P(("wide", "narrow"), None),
        check_vma=False,
    )
```

```python
import jax
import jax.numpy as jnp
from jax import lax
from jax.experimental import pallas as pl
from jax.experimental.pallas import tpu as pltpu
from jax.sharding import PartitionSpec as P

MESH = pl.DeviceIdType.MESH
BF = jnp.bfloat16
F32 = jnp.float32
SCALE = 0.125
LOW = -1e30


def iota(shape, dim):
    return lax.broadcasted_iota(jnp.int32, shape, dim)


def tile_of_row(r, core):
    j = r % 32
    s = jnp.where(j == 1, 16, jnp.where((j >= 2) & (j <= 16), j - 1, j))
    return 16 * s + 4 * ((r // 32) % 4) + 2 * ((r // 256 + core) % 2) + (r // 128) % 2


def dot(a, b):
    return jnp.dot(a, b, preferred_element_type=F32)


def dot_t(a, b):
    return lax.dot_general(a, b, (((1,), (1,)), ((), ())), preferred_element_type=F32)


def soft(q, k, v, mask=None):
    s = dot_t(q, k) * SCALE
    if mask is not None:
        s = jnp.where(mask, s, LOW)
    peak = jnp.max(s, axis=-1, keepdims=True)
    w = jnp.exp(s - peak)
    return peak, jnp.sum(w, axis=-1, keepdims=True), dot(w.astype(BF), v)


def merge(a, b):
    top = jnp.maximum(a[0], b[0])
    ea, eb = jnp.exp(a[0] - top), jnp.exp(b[0] - top)
    return top, a[1] * ea + b[1] * eb, a[2] * ea + b[2] * eb


def kernel(
    tok_hbm, wp_hbm, wo_hbm, out_ref,
    tok, perm, back, xs, xo, wp, wo, qkv, kv2, kv3, q3, part_out, part_in, att, got, y,
    loc_sem, ws, wr, os_, or_, s2, r2, s3, r3, sc, rc,
):
    w, n = lax.axis_index("wide"), lax.axis_index("narrow")
    x, yl, core, z, yh = n % 4, n // 4, w % 2, (w // 2) % 8, w // 16
    yy = 2 * yh + yl

    def dev(dx=0, dy=0, dz=0, dc=0):
        y_ = (yy + dy) % 8
        return ((y_ // 2) * 16 + ((z + dz) % 8) * 2 + (core + dc) % 2, (y_ % 2) * 4 + (x + dx) % 4)

    barrier = pltpu.get_barrier_semaphore()
    partners = (
        [dev(dx=k) for k in (1, 2, 3)] + [dev(dy=k) for k in range(1, 8)] + [dev(dz=k) for k in range(1, 8)] + [dev(dc=1)]
    )
    for p in partners:
        pl.semaphore_signal(barrier, inc=1, device_id=p, device_id_type=MESH)

    def send(src, dst, ss, rs, to):
        c = pltpu.make_async_remote_copy(
            src_ref=src, dst_ref=dst, send_sem=ss, recv_sem=rs, device_id=to, device_id_type=MESH
        )
        c.start()
        return c

    mine = pl.ds(pl.multiple_of(96 * n, 32), 96)
    loc = [
        pltpu.make_async_copy(tok_hbm, tok, loc_sem.at[0]),
        pltpu.make_async_copy(wo_hbm, wo.at[mine], loc_sem.at[1]),
    ]
    for m in range(3):
        for t in range(3):
            src = wp_hbm.at[:, pl.ds(pl.multiple_of(768 * m + 256 * t + 128 * core, 128), 128)]
            dst = wp.at[mine, pl.ds(384 * m + 128 * t, 128)]
            loc.append(pltpu.make_async_copy(src, dst, loc_sem.at[2 + 3 * m + t]))
    for c in loc[2:] + loc[:2]:
        c.start()
    perm[...] = jnp.where(iota((512, 512), 1) == tile_of_row(iota((512, 1), 0), core), 1.0, 0.0).astype(BF)
    back[...] = jnp.where(iota((512, 512), 0) == tile_of_row(iota((1, 512), 1), core), 1.0, 0.0).astype(BF)
    for c in loc[2:]:
        c.wait()
    pl.semaphore_wait(barrier, len(partners))

    class Rows:
        def __init__(self, m, ss, rs):
            self.cols, self.ss, self.rs = pl.ds(384 * m, 384), ss, rs
            self.sent = []

        def go(self, dx, other, first, count, to):
            j = ((1 - yl) if other else yl) * 4 + (x + dx) % 4
            ref = wp.at[pl.ds(pl.multiple_of(96 * j + first, 16), count), self.cols]
            k = len(self.sent)
            c = send(ref, ref, self.ss.at[k], self.rs.at[k], to)
            self.sent.append(c)
            return c

        def phase_a(self):
            self.a = [self.go(0, False, 0, 96, dev(dx=1)), self.go(0, False, 0, 96, dev(dx=3))]
            self.a += [self.go(0, False, 0, 48, dev(dy=1)), self.go(0, False, 48, 48, dev(dy=7))]

        def phase_b(self):
            self.a[0].wait_recv()
            b1, b3 = self.go(3, False, 0, 48, dev(dx=1)), self.go(3, False, 0, 96, dev(dy=1))
            self.a[1].wait_recv()
            b2, b4 = self.go(1, False, 48, 48, dev(dx=3)), self.go(1, False, 0, 96, dev(dy=7))
            self.b = [b1, b2, b3, b4]

        def phase_c(self):
            b1, b2, b3, b4 = self.b
            b1.wait_recv()
            c3 = self.go(2, False, 0, 16, dev(dy=1))
            b2.wait_recv()
            c4 = self.go(2, False, 64, 32, dev(dy=7))
            b3.wait_recv()
            c1 = self.go(3, True, 16, 32, dev(dx=1))
            b4.wait_recv()
            c2 = self.go(1, True, 48, 16, dev(dx=3))
            self.c = [c1, c2, c3, c4]

        def finish(self):
            for c in self.a[2:] + self.c:
                c.wait_recv()

    class Twin:
        def __init__(self):
            self.sent, self.passed = [], []
            self.left, self.right, self.full = pl.ds(0, 384), pl.ds(384, 384), pl.ds(0, 768)

        def at(self, dx, other, cols):
            j = ((1 - yl) if other else yl) * 4 + (x + dx) % 4
            return wo.at[pl.ds(pl.multiple_of(96 * j + 48 * core, 16), 48), cols]

        def go(self, ref, to):
            k = len(self.sent)
            c = send(ref, ref, os_.at[k], or_.at[k], to)
            self.sent.append(c)
            return c

        def twin(self, *refs):
            for ref in refs:
                self.passed.append(self.go(ref, dev(dc=1)))

        def phase_ax(self):
            self.a = [self.go(self.at(0, False, self.full), dev(dx=k)) for k in (1, 3, 2)]

        def phase_ay(self):
            self.a.append(self.go(self.at(0, False, self.left), dev(dy=1)))
            self.a.append(self.go(self.at(0, False, self.right), dev(dy=7)))

        def phase_b(self):
            a = self.a
            a[0].wait_recv()
            self.b = [self.go(self.at(3, False, self.full), dev(dy=1))]
            a[1].wait_recv()
            self.b.append(self.go(self.at(1, False, self.full), dev(dy=7)))
            a[2].wait_recv()
            self.b.append(self.go(self.at(2, False, self.left), dev(dy=1)))
            self.b.append(self.go(self.at(2, False, self.right), dev(dy=7)))
            self.twin(*[self.at(k, False, self.full) for k in (1, 2, 3)])
            a[3].wait_recv()
            a[4].wait_recv()
            self.twin(self.at(0, True, self.full))

        def phase_c(self):
            for c in self.b:
                c.wait_recv()
            self.twin(*[self.at(k, True, self.full) for k in (1, 2, 3)])

        def finish(self):
            for c in self.passed:
                c.wait_recv()

    gq, gk, gv = (Rows(m, ws.at[m], wr.at[m]) for m in range(3))
    outp = Twin()
    weights = (gk, gv, gq)
    for g in weights:
        g.phase_a()
    loc[0].wait()
    xo[...] = dot(perm[256:, :], tok[...]).astype(BF)
    tokens_sent = send(xo, xs.at[pl.ds(256, 256)], sc.at[0], rc.at[0], dev(dc=1))
    gk.phase_b()
    xs[:256, :] = dot(perm[:256, :], tok[...]).astype(BF)
    gv.phase_b()
    gq.phase_b()
    for g in weights:
        g.phase_c()

    def project(m):
        qkv[:, 384 * m : 384 * m + 384] = dot(xs[...], wp[:, 384 * m : 384 * m + 384]).astype(BF)

    low = iota((1, 128), 1) < 64
    row16 = iota((16, 128), 0)
    zeros8 = jnp.zeros((8, 128), F32)
    mine2 = pl.ds(pl.multiple_of(32 * n, 32), 32)

    def second(m, e, t):
        a = 256 * e + 32 * t
        c = 384 * m + 128 * t
        return jnp.where(low, qkv[a : a + 32, c : c + 128].astype(F32), qkv[a + 128 : a + 160, c : c + 128].astype(F32))

    def third(m):
        out = jnp.zeros((16, 128), F32)
        for e in range(2):
            for t in range(3):
                v = second(m, e, t)
                i = 4 * t + 2 * e
                if m > 0:
                    kv2[m - 1, e, mine2, 128 * t : 128 * t + 128] = v.astype(BF)
                u = jnp.concatenate([v[:8], zeros8], axis=0)
                if i:
                    u = pltpu.roll(u, i, 0)
                out = jnp.where((row16 >= i) & (row16 < i + 2), u, out)
        if m > 0:
            kv3[m - 1, x, yy] = out.astype(BF)
        else:
            q3[z] = out.astype(BF)

    tokens_sent.wait_recv()
    gk.finish()
    project(1)
    third(1)
    gv.finish()
    project(2)
    third(2)

    sent = [tokens_sent]
    k2 = k3 = 0

    def go3(src, dst, to):
        nonlocal k3
        c = send(src, dst, s3.at[k3], r3.at[k3], to)
        k3 += 1
        sent.append(c)
        return c

    def go2(ref, to):
        nonlocal k2
        c = send(ref, ref, s2.at[k2], r2.at[k2], to)
        k2 += 1
        sent.append(c)
        return c

    def at2(dx, other, e=None):
        j = ((1 - yl) if other else yl) * 4 + (x + dx) % 4
        return kv2.at[:, pl.ds(0, 2) if e is None else pl.ds(e, 1), pl.ds(pl.multiple_of(32 * j, 32), 32)]

    own3 = kv3.at[:, x, yy]
    a3 = [go3(own3, own3, dev(dy=k)) for k in (4, 3, 5, 2, 6, 1, 7)]
    pair = (w, (1 - yl) * 4 + x)
    u = [go2(at2(0, False), to) for to in (dev(dx=1), dev(dx=3))]
    loc[1].wait()
    outp.phase_ax()

    gq.finish()
    project(0)
    third(0)
    sq = [go3(q3.at[z], q3.at[z], dev(dz=k)) for k in (4, 3, 5, 2, 6, 1, 7)]

    first = {}

    def level1(e, t):
        o = []
        for lo in range(2):
            r = slice(256 * e + 128 * lo, 256 * e + 128 * lo + 128)
            q = jnp.where(low if lo == 0 else ~low, qkv[r, 128 * t : 128 * t + 128].astype(F32), 0.0).astype(BF)
            pk, tot, num = soft(q, qkv[r, 384 + 128 * t : 512 + 128 * t], qkv[r, 768 + 128 * t : 896 + 128 * t])
            o.append(num / tot)
            b = slice(32 * t, 32 * t + 32)
            first[e, t, lo] = pk[b], tot[b], num[b]
        att[e, :, 128 * t : 128 * t + 128] = jnp.where(low, o[0], o[1]).astype(BF)

    level1(0, 0)
    for c in a3:
        c.wait_recv()
    plane = kv3.at[:, x]
    b3 = [go3(plane, plane, dev(dx=k)) for k in (2, 1, 3)]
    u.append(go2(at2(0, False), pair))
    outp.phase_ay()
    u[0].wait_recv()
    v1 = go2(at2(3, False, 0), dev(dx=1))
    u[1].wait_recv()
    v2 = go2(at2(1, False, 1), dev(dx=3))
    level1(0, 1)
    level1(0, 2)
    u[2].wait_recv()
    g2 = [go2(at2(0, True), dev(dx=1)), go2(at2(0, True), dev(dx=3))]
    for c in b3 + sq:
        c.wait_recv()

    qa = q3[...].reshape(128, 128).astype(F32)
    qs = jnp.concatenate([jnp.where(low, qa, 0.0), jnp.where(low, 0.0, qa)], axis=0).astype(BF)
    same = (iota((256, 512), 0) % 16) // 4 == (iota((256, 512), 1) % 16) // 4
    pk, tot, num = soft(qs, kv3[0].reshape(512, 128), kv3[1].reshape(512, 128), same)
    num = jnp.where(low, num[:128], num[128:]).reshape(8, 16, 128)
    row, lane = iota((8, 16, 128), 1), iota((8, 16, 128), 2)

    def to_lanes(v):
        a, b = v[:128].reshape(8, 16, 1), v[128:].reshape(8, 16, 1)
        u = jnp.where(lane == row, a, jnp.where(lane == row + 64, b, 0.0))
        return jnp.sum(u, axis=1, keepdims=True)

    part_out[...] = jnp.where(row < 12, num, jnp.where(row == 12, to_lanes(pk), to_lanes(tot)))
    sp = [go3(part_out.at[(z + k) % 8], part_in.at[z], dev(dz=k)) for k in (4, 3, 5, 2, 6, 1, 7)]
    part_in[z] = part_out[z]
    v1.wait_recv()
    v2.wait_recv()
    g2.append(go2(at2(2, False), pair))
    outp.phase_b()
    for t in range(3):
        level1(1, t)
    outp.phase_c()

    for c in g2:
        c.wait_recv()
    both = {}
    for e in range(2):
        for t in range(3):
            v = second(0, e, t)
            q = jnp.concatenate([jnp.where(low, v, 0.0), jnp.where(low, 0.0, v)], axis=0).astype(BF)
            pk, tot, num = soft(q, kv2[0, e, :, 128 * t : 128 * t + 128], kv2[1, e, :, 128 * t : 128 * t + 128])
            for lo in range(2):
                b = slice(32 * lo, 32 * lo + 32)
                both[e, t, lo] = merge(first[e, t, lo], (pk[b], tot[b], num[b]))

    outp.finish()
    for c in sp:
        c.wait_recv()
    p = part_in[...]

    def from_lanes(v):
        a = jnp.sum(jnp.where(lane == row, v, 0.0), axis=-1, keepdims=True)
        b = jnp.sum(jnp.where(lane == row + 64, v, 0.0), axis=-1, keepdims=True)
        return jnp.where(lane < 64, a, b)

    pk, tot = from_lanes(p[:, 12:13]), from_lanes(p[:, 13:14])
    top = jnp.max(pk, axis=0)
    f = jnp.exp(pk - top[None])
    dist = (top, jnp.sum(tot * f, axis=0), jnp.sum(p * f, axis=0))

    use = iota((8, 128), 0) < 2

    def complete(e):
        for t in range(3):
            i = 4 * t + 2 * e
            d = [pltpu.roll(v, 16 - i, 0)[:8] if i else v[:8] for v in dist]
            d = (jnp.where(use, d[0], LOW), jnp.where(use, d[1], 0.0), jnp.where(use, d[2], 0.0))
            o = []
            for lo in range(2):
                pk, tot, num = both[e, t, lo]
                _, tot8, num8 = merge((pk[:8], tot[:8], num[:8]), d)
                o.append(jnp.concatenate([num8 / tot8, num[8:] / tot[8:]], axis=0))
            att[e, 32 * t : 32 * t + 32, 128 * t : 128 * t + 128] = jnp.where(low, o[0], o[1]).astype(BF)

    low384 = iota((1, 384), 1) % 128 < 64

    def output(e, packed):
        v = packed.astype(F32)
        rows = jnp.concatenate([jnp.where(low384, v, 0.0), jnp.where(low384, 0.0, v)], axis=0).astype(BF)
        at = [256 * t + 128 * ((core + e) % 2) for t in range(3)]
        wc = jnp.concatenate([wo[pl.ds(pl.multiple_of(a, 128), 128), :] for a in at], axis=0)
        y[256 * e : 256 * e + 256, :] = dot(rows, wc).astype(BF)

    complete(1)
    swap = send(att.at[1], got, sc.at[1], rc.at[1], dev(dc=1))
    sent.append(swap)
    complete(0)
    output(0, att[0])
    swap.wait_recv()
    output(1, got[...])
    out_ref[...] = dot(back[...], y[...]).astype(BF)
    for g in weights + (outp,):
        sent += g.sent
    for c in sent:
        c.wait_send()


def shards(tokens, proj_weight, out_weight):
    hbm = pl.BlockSpec(memory_space=pl.ANY)
    dma = pltpu.SemaphoreType.DMA
    return pl.pallas_call(
        kernel,
        out_shape=jax.ShapeDtypeStruct((512, 768), BF),
        in_specs=[hbm] * 3,
        out_specs=pl.BlockSpec(memory_space=pltpu.VMEM),
        scratch_shapes=[
            pltpu.VMEM((512, 768), BF),
            pltpu.VMEM((512, 512), BF),
            pltpu.VMEM((512, 512), BF),
            pltpu.VMEM((512, 768), BF),
            pltpu.VMEM((256, 768), BF),
            pltpu.VMEM((768, 1152), BF),
            pltpu.VMEM((768, 768), BF),
            pltpu.VMEM((512, 1152), BF),
            pltpu.VMEM((2, 2, 256, 384), BF),
            pltpu.VMEM((2, 4, 8, 16, 128), BF),
            pltpu.VMEM((8, 16, 128), BF),
            pltpu.VMEM((8, 16, 128), F32),
            pltpu.VMEM((8, 16, 128), F32),
            pltpu.VMEM((2, 128, 384), BF),
            pltpu.VMEM((128, 384), BF),
            pltpu.VMEM((512, 768), BF),
            dma((11,)),
            dma((3, 12)), dma((3, 12)), dma((16,)), dma((16,)),
            dma((8,)), dma((8,)), dma((24,)), dma((24,)), dma((2,)), dma((2,)),
        ],
        compiler_params=pltpu.CompilerParams(collective_id=0, has_side_effects=True, vmem_limit_bytes=56 << 20),
    )(tokens, proj_weight, out_weight)


def solution(mesh):
    return jax.shard_map(
        shards,
        mesh=mesh,
        in_specs=(P(("wide", "narrow"), None), P("narrow", None), P("narrow", None)),
        out_specs=P(("wide", "narrow"), None),
        check_vma=False,
    )
```

```python
import jax
import jax.numpy as jnp
from jax import lax
from jax.experimental import pallas as pl
from jax.experimental.pallas import tpu as pltpu
from jax.sharding import PartitionSpec as P

MESH = pl.DeviceIdType.MESH
BF = jnp.bfloat16
F32 = jnp.float32
SCALE = 0.125
LOW = -1e30


def iota(shape, dim):
    return lax.broadcasted_iota(jnp.int32, shape, dim)


def tile_of_row(r, core):
    j = r % 32
    s = jnp.where(j == 1, 16, jnp.where((j >= 2) & (j <= 16), j - 1, j))
    return 16 * s + 4 * ((r // 32) % 4) + 2 * ((r // 256 + core) % 2) + (r // 128) % 2


def dot(a, b):
    return jnp.dot(a, b, preferred_element_type=F32)


def dot_t(a, b):
    return lax.dot_general(a, b, (((1,), (1,)), ((), ())), preferred_element_type=F32)


def soft(q, k, v, mask=None):
    s = dot_t(q, k) * SCALE
    if mask is not None:
        s = jnp.where(mask, s, LOW)
    peak = jnp.max(s, axis=-1, keepdims=True)
    w = jnp.exp(s - peak)
    return peak, jnp.sum(w, axis=-1, keepdims=True), dot(w.astype(BF), v)


def merge(a, b):
    top = jnp.maximum(a[0], b[0])
    ea, eb = jnp.exp(a[0] - top), jnp.exp(b[0] - top)
    return top, a[1] * ea + b[1] * eb, a[2] * ea + b[2] * eb


def kernel(
    tok_hbm, wp_hbm, wo_hbm, y,
    tok, perm, xs, xo, wp, wo, qkv, kv2, kv3, q3, part_out, part_in, att, got,
    loc_sem, ws, wr, os_, or_, s2, r2, s3, r3, sc, rc,
):
    w, n = lax.axis_index("wide"), lax.axis_index("narrow")
    x, yl, core, z, yh = n % 4, n // 4, w % 2, (w // 2) % 8, w // 16
    yy = 2 * yh + yl

    def dev(dx=0, dy=0, dz=0, dc=0):
        y_ = (yy + dy) % 8
        return ((y_ // 2) * 16 + ((z + dz) % 8) * 2 + (core + dc) % 2, (y_ % 2) * 4 + (x + dx) % 4)

    barrier = pltpu.get_barrier_semaphore()
    partners = (
        [dev(dx=k) for k in (1, 2, 3)] + [dev(dy=k) for k in range(1, 8)] + [dev(dz=k) for k in range(1, 8)] + [dev(dc=1)]
    )
    for p in partners:
        pl.semaphore_signal(barrier, inc=1, device_id=p, device_id_type=MESH)

    def send(src, dst, ss, rs, to):
        c = pltpu.make_async_remote_copy(
            src_ref=src, dst_ref=dst, send_sem=ss, recv_sem=rs, device_id=to, device_id_type=MESH
        )
        c.start()
        return c

    mine = pl.ds(pl.multiple_of(96 * n, 32), 96)
    loc = [
        pltpu.make_async_copy(tok_hbm, tok, loc_sem.at[0]),
        pltpu.make_async_copy(wo_hbm, wo.at[mine], loc_sem.at[1]),
    ]
    for m in range(3):
        for t in range(3):
            src = wp_hbm.at[:, pl.ds(pl.multiple_of(768 * m + 256 * t + 128 * core, 128), 128)]
            dst = wp.at[m, mine, pl.ds(128 * t, 128)]
            loc.append(pltpu.make_async_copy(src, dst, loc_sem.at[2 + 3 * m + t]))
    for c in loc[2:] + loc[:2]:
        c.start()
    perm[...] = jnp.where(iota((512, 512), 1) == tile_of_row(iota((512, 1), 0), core), 1.0, 0.0).astype(BF)
    for c in loc[2:]:
        c.wait()
    pl.semaphore_wait(barrier, len(partners))

    class Rows:
        def __init__(self, m, ss, rs):
            self.buf, self.ss, self.rs = wp.at[m], ss, rs
            self.sent = []

        def go(self, dx, other, first, count, to):
            j = ((1 - yl) if other else yl) * 4 + (x + dx) % 4
            ref = self.buf.at[pl.ds(pl.multiple_of(96 * j + first, 16), count)]
            k = len(self.sent)
            c = send(ref, ref, self.ss.at[k], self.rs.at[k], to)
            self.sent.append(c)
            return c

        def phase_a(self):
            self.a = [self.go(0, False, 0, 96, dev(dx=k)) for k in (1, 3, 2)]
            self.a += [self.go(0, False, 0, 48, dev(dy=1)), self.go(0, False, 48, 48, dev(dy=7))]

        def phase_b(self):
            self.a[0].wait_recv()
            self.b = [self.go(3, False, 0, 96, dev(dy=1))]
            self.a[1].wait_recv()
            self.b.append(self.go(1, False, 0, 96, dev(dy=7)))
            self.a[2].wait_recv()
            self.b += [self.go(2, False, 0, 48, dev(dy=1)), self.go(2, False, 48, 48, dev(dy=7))]

        def finish(self):
            for c in self.a[3:] + self.b:
                c.wait_recv()

    class Twin:
        def __init__(self):
            self.sent, self.passed = [], []
            self.left, self.right, self.full = pl.ds(0, 384), pl.ds(384, 384), pl.ds(0, 768)

        def at(self, dx, other, cols):
            j = ((1 - yl) if other else yl) * 4 + (x + dx) % 4
            return wo.at[pl.ds(pl.multiple_of(96 * j + 48 * core, 16), 48), cols]

        def go(self, ref, to):
            k = len(self.sent)
            c = send(ref, ref, os_.at[k], or_.at[k], to)
            self.sent.append(c)
            return c

        def twin(self, *refs):
            for ref in refs:
                self.passed.append(self.go(ref, dev(dc=1)))

        def phase_ax(self):
            self.a = [self.go(self.at(0, False, self.full), dev(dx=k)) for k in (1, 3, 2)]

        def phase_ay(self):
            self.a.append(self.go(self.at(0, False, self.left), dev(dy=1)))
            self.a.append(self.go(self.at(0, False, self.right), dev(dy=7)))

        def phase_b(self):
            a = self.a
            a[0].wait_recv()
            self.b = [self.go(self.at(3, False, self.full), dev(dy=1))]
            a[1].wait_recv()
            self.b.append(self.go(self.at(1, False, self.full), dev(dy=7)))
            a[2].wait_recv()
            self.b.append(self.go(self.at(2, False, self.left), dev(dy=1)))
            self.b.append(self.go(self.at(2, False, self.right), dev(dy=7)))
            self.twin(*[self.at(k, False, self.full) for k in (1, 2, 3)])
            a[3].wait_recv()
            a[4].wait_recv()
            self.twin(self.at(0, True, self.full))

        def phase_c(self):
            for c in self.b:
                c.wait_recv()
            self.twin(*[self.at(k, True, self.full) for k in (1, 2, 3)])

        def finish(self):
            for c in self.passed:
                c.wait_recv()

    gq, gk, gv = (Rows(m, ws.at[m], wr.at[m]) for m in range(3))
    outp = Twin()
    weights = (gk, gv, gq)
    for g in weights:
        g.phase_a()
    loc[0].wait()
    xo[...] = dot(perm[256:, :], tok[...]).astype(BF)
    tokens_sent = send(xo, xs.at[pl.ds(256, 256)], sc.at[0], rc.at[0], dev(dc=1))
    gk.phase_b()
    xs[:256, :] = dot(perm[:256, :], tok[...]).astype(BF)
    gv.phase_b()
    gq.phase_b()
    loc[1].wait()
    outp.phase_ax()
    outp.phase_ay()

    def project(m):
        qkv[:, 384 * m : 384 * m + 384] = dot(xs[...], wp[m]).astype(BF)

    low = iota((1, 128), 1) < 64
    row16 = iota((16, 128), 0)
    zeros8 = jnp.zeros((8, 128), F32)
    mine2 = pl.ds(pl.multiple_of(32 * n, 32), 32)

    def second(m, e, t):
        a = 256 * e + 32 * t
        c = 384 * m + 128 * t
        return jnp.where(low, qkv[a : a + 32, c : c + 128].astype(F32), qkv[a + 128 : a + 160, c : c + 128].astype(F32))

    def third(m):
        out = jnp.zeros((16, 128), F32)
        for e in range(2):
            for t in range(3):
                v = second(m, e, t)
                i = 4 * t + 2 * e
                if m > 0:
                    kv2[m - 1, e, mine2, 128 * t : 128 * t + 128] = v.astype(BF)
                u = jnp.concatenate([v[:8], zeros8], axis=0)
                if i:
                    u = pltpu.roll(u, i, 0)
                out = jnp.where((row16 >= i) & (row16 < i + 2), u, out)
        if m > 0:
            kv3[m - 1, x, yy] = out.astype(BF)
        else:
            q3[z] = out.astype(BF)

    tokens_sent.wait_recv()
    gk.finish()
    project(1)
    third(1)
    gv.finish()
    project(2)
    third(2)

    sent = [tokens_sent]
    k2 = k3 = 0

    def go3(src, dst, to):
        nonlocal k3
        c = send(src, dst, s3.at[k3], r3.at[k3], to)
        k3 += 1
        sent.append(c)
        return c

    def go2(ref, to):
        nonlocal k2
        c = send(ref, ref, s2.at[k2], r2.at[k2], to)
        k2 += 1
        sent.append(c)
        return c

    def at2(dx, other, e=None):
        j = ((1 - yl) if other else yl) * 4 + (x + dx) % 4
        return kv2.at[:, pl.ds(0, 2) if e is None else pl.ds(e, 1), pl.ds(pl.multiple_of(32 * j, 32), 32)]

    own3 = kv3.at[:, x, yy]
    a3 = [go3(own3, own3, dev(dy=k)) for k in (4, 3, 5, 2, 6, 1, 7)]
    pair = (w, (1 - yl) * 4 + x)
    u = [go2(at2(0, False), to) for to in (dev(dx=1), dev(dx=3))]
    gq.finish()
    project(0)
    third(0)
    sq = [go3(q3.at[z], q3.at[z], dev(dz=k)) for k in (4, 3, 5, 2, 6, 1, 7)]
    u.append(go2(at2(0, False), pair))

    first = {}

    def level1(e, t):
        o = []
        for lo in range(2):
            r = slice(256 * e + 128 * lo, 256 * e + 128 * lo + 128)
            q = jnp.where(low if lo == 0 else ~low, qkv[r, 128 * t : 128 * t + 128].astype(F32), 0.0).astype(BF)
            pk, tot, num = soft(q, qkv[r, 384 + 128 * t : 512 + 128 * t], qkv[r, 768 + 128 * t : 896 + 128 * t])
            o.append(num / tot)
            b = slice(32 * t, 32 * t + 32)
            first[e, t, lo] = pk[b], tot[b], num[b]
        att[e, :, 128 * t : 128 * t + 128] = jnp.where(low, o[0], o[1]).astype(BF)

    for c in a3:
        c.wait_recv()
    plane = kv3.at[:, x]
    b3 = [go3(plane, plane, dev(dx=k)) for k in (2, 1, 3)]
    u[0].wait_recv()
    v1 = go2(at2(3, False, 0), dev(dx=1))
    u[1].wait_recv()
    v2 = go2(at2(1, False, 1), dev(dx=3))
    outp.phase_b()
    level1(0, 0)
    level1(0, 1)
    u[2].wait_recv()
    g2 = [go2(at2(0, True), dev(dx=1)), go2(at2(0, True), dev(dx=3))]
    for c in b3 + sq:
        c.wait_recv()

    qa = q3[...].reshape(128, 128).astype(F32)
    qs = jnp.concatenate([jnp.where(low, qa, 0.0), jnp.where(low, 0.0, qa)], axis=0).astype(BF)
    same = (iota((256, 512), 0) % 16) // 4 == (iota((256, 512), 1) % 16) // 4
    pk, tot, num = soft(qs, kv3[0].reshape(512, 128), kv3[1].reshape(512, 128), same)
    num = jnp.where(low, num[:128], num[128:]).reshape(8, 16, 128)
    row, lane = iota((8, 16, 128), 1), iota((8, 16, 128), 2)

    def to_lanes(v):
        a, b = v[:128].reshape(8, 16, 1), v[128:].reshape(8, 16, 1)
        u = jnp.where(lane == row, a, jnp.where(lane == row + 64, b, 0.0))
        return jnp.sum(u, axis=1, keepdims=True)

    part_out[...] = jnp.where(row < 12, num, jnp.where(row == 12, to_lanes(pk), to_lanes(tot)))
    sp = [go3(part_out.at[(z + k) % 8], part_in.at[z], dev(dz=k)) for k in (4, 3, 5, 2, 6, 1, 7)]
    part_in[z] = part_out[z]
    v1.wait_recv()
    v2.wait_recv()
    g2.append(go2(at2(2, False), pair))
    level1(0, 2)
    for t in range(3):
        level1(1, t)
    outp.phase_c()

    for c in g2:
        c.wait_recv()
    both = {}
    for e in range(2):
        for t in range(3):
            v = second(0, e, t)
            q = jnp.concatenate([jnp.where(low, v, 0.0), jnp.where(low, 0.0, v)], axis=0).astype(BF)
            pk, tot, num = soft(q, kv2[0, e, :, 128 * t : 128 * t + 128], kv2[1, e, :, 128 * t : 128 * t + 128])
            for lo in range(2):
                b = slice(32 * lo, 32 * lo + 32)
                both[e, t, lo] = merge(first[e, t, lo], (pk[b], tot[b], num[b]))

    outp.finish()
    for c in sp:
        c.wait_recv()
    p = part_in[...]

    def from_lanes(v):
        a = jnp.sum(jnp.where(lane == row, v, 0.0), axis=-1, keepdims=True)
        b = jnp.sum(jnp.where(lane == row + 64, v, 0.0), axis=-1, keepdims=True)
        return jnp.where(lane < 64, a, b)

    pk, tot = from_lanes(p[:, 12:13]), from_lanes(p[:, 13:14])
    top = jnp.max(pk, axis=0)
    f = jnp.exp(pk - top[None])
    dist = (top, jnp.sum(tot * f, axis=0), jnp.sum(p * f, axis=0))

    use = iota((8, 128), 0) < 2

    def complete(e):
        for t in range(3):
            i = 4 * t + 2 * e
            d = [pltpu.roll(v, 16 - i, 0)[:8] if i else v[:8] for v in dist]
            d = (jnp.where(use, d[0], LOW), jnp.where(use, d[1], 0.0), jnp.where(use, d[2], 0.0))
            o = []
            for lo in range(2):
                pk, tot, num = both[e, t, lo]
                _, tot8, num8 = merge((pk[:8], tot[:8], num[:8]), d)
                o.append(jnp.concatenate([num8 / tot8, num[8:] / tot[8:]], axis=0))
            att[e, 32 * t : 32 * t + 32, 128 * t : 128 * t + 128] = jnp.where(low, o[0], o[1]).astype(BF)

    low384 = iota((1, 384), 1) % 128 < 64

    def output(e, packed):
        v = packed.astype(F32)
        rows = jnp.concatenate([jnp.where(low384, v, 0.0), jnp.where(low384, 0.0, v)], axis=0).astype(BF)
        at = [256 * t + 128 * ((core + e) % 2) for t in range(3)]
        wc = jnp.concatenate([wo[pl.ds(pl.multiple_of(a, 128), 128), :] for a in at], axis=0)
        y[256 * e : 256 * e + 256, :] = dot(rows, wc).astype(BF)

    complete(1)
    swap = send(att.at[1], got, sc.at[1], rc.at[1], dev(dc=1))
    sent.append(swap)
    complete(0)
    output(0, att[0])
    swap.wait_recv()
    output(1, got[...])
    for g in weights + (outp,):
        sent += g.sent
    for c in sent:
        c.wait_send()


def in_order(y, out_ref):
    core = lax.axis_index("wide") % 2
    p = iota((256, 512), 0) + 256 * pl.program_id(0)
    back = jnp.where(p == tile_of_row(iota((1, 512), 1), core), 1.0, 0.0).astype(BF)
    out_ref[...] = dot(back, y[...]).astype(BF)


def shards(tokens, proj_weight, out_weight):
    hbm = pl.BlockSpec(memory_space=pl.ANY)
    dma = pltpu.SemaphoreType.DMA
    rows = pl.pallas_call(
        kernel,
        out_shape=jax.ShapeDtypeStruct((512, 768), BF),
        in_specs=[hbm] * 3,
        out_specs=pl.BlockSpec(memory_space=pltpu.VMEM),
        scratch_shapes=[
            pltpu.VMEM((512, 768), BF),
            pltpu.VMEM((512, 512), BF),
            pltpu.VMEM((512, 768), BF),
            pltpu.VMEM((256, 768), BF),
            pltpu.VMEM((3, 768, 384), BF),
            pltpu.VMEM((768, 768), BF),
            pltpu.VMEM((512, 1152), BF),
            pltpu.VMEM((2, 2, 256, 384), BF),
            pltpu.VMEM((2, 4, 8, 16, 128), BF),
            pltpu.VMEM((8, 16, 128), BF),
            pltpu.VMEM((8, 16, 128), F32),
            pltpu.VMEM((8, 16, 128), F32),
            pltpu.VMEM((2, 128, 384), BF),
            pltpu.VMEM((128, 384), BF),
            dma((11,)),
            dma((3, 12)), dma((3, 12)), dma((16,)), dma((16,)),
            dma((8,)), dma((8,)), dma((24,)), dma((24,)), dma((2,)), dma((2,)),
        ],
        compiler_params=pltpu.CompilerParams(collective_id=0, has_side_effects=True, vmem_limit_bytes=56 << 20),
    )(tokens, proj_weight, out_weight)
    return pl.pallas_call(
        in_order,
        out_shape=jax.ShapeDtypeStruct((512, 768), BF),
        grid=(2,),
        in_specs=[pl.BlockSpec((512, 768), lambda i: (0, 0))],
        out_specs=pl.BlockSpec((256, 768), lambda i: (i, 0)),
        compiler_params=pltpu.CompilerParams(vmem_limit_bytes=16 << 20),
    )(rows)


def solution(mesh):
    return jax.shard_map(
        shards,
        mesh=mesh,
        in_specs=(P(("wide", "narrow"), None), P("narrow", None), P("narrow", None)),
        out_specs=P(("wide", "narrow"), None),
        check_vma=False,
    )
```

```python
import jax
import jax.numpy as jnp
from jax import lax
from jax.experimental import pallas as pl
from jax.experimental.pallas import tpu as pltpu
from jax.sharding import PartitionSpec as P

MESH = pl.DeviceIdType.MESH
BF = jnp.bfloat16
F32 = jnp.float32
SCALE = 0.125
LOW = -1e30


def iota(shape, dim):
    return lax.broadcasted_iota(jnp.int32, shape, dim)


def tile_of_row(r, core):
    j = r % 32
    s = jnp.where(j == 1, 16, jnp.where((j >= 2) & (j <= 16), j - 1, j))
    return 16 * s + 4 * ((r // 32) % 4) + 2 * ((r // 256 + core) % 2) + (r // 128) % 2


def dot(a, b):
    return jnp.dot(a, b, preferred_element_type=F32)


def dot_t(a, b):
    return lax.dot_general(a, b, (((1,), (1,)), ((), ())), preferred_element_type=F32)


def soft(q, k, v, mask=None):
    s = dot_t(q, k) * SCALE
    if mask is not None:
        s = jnp.where(mask, s, LOW)
    peak = jnp.max(s, axis=-1, keepdims=True)
    w = jnp.exp(s - peak)
    return peak, jnp.sum(w, axis=-1, keepdims=True), dot(w.astype(BF), v)


def merge(a, b):
    top = jnp.maximum(a[0], b[0])
    ea, eb = jnp.exp(a[0] - top), jnp.exp(b[0] - top)
    return top, a[1] * ea + b[1] * eb, a[2] * ea + b[2] * eb


def kernel(
    tok_hbm, wp_hbm, wo_hbm, y,
    tok, perm, xs, xo, wp, wo, qkv, kv2, kv3, q3, part_out, part_in, att, got,
    loc_sem, ws, wr, os_, or_, s2, r2, s3, r3, sc, rc,
):
    w, n = lax.axis_index("wide"), lax.axis_index("narrow")
    x, yl, core, z, yh = n % 4, n // 4, w % 2, (w // 2) % 8, w // 16
    yy = 2 * yh + yl

    def dev(dx=0, dy=0, dz=0, dc=0):
        y_ = (yy + dy) % 8
        return ((y_ // 2) * 16 + ((z + dz) % 8) * 2 + (core + dc) % 2, (y_ % 2) * 4 + (x + dx) % 4)

    barrier = pltpu.get_barrier_semaphore()
    partners = (
        [dev(dx=k) for k in (1, 2, 3)] + [dev(dy=k) for k in range(1, 8)] + [dev(dz=k) for k in range(1, 8)] + [dev(dc=1)]
    )
    for p in partners:
        pl.semaphore_signal(barrier, inc=1, device_id=p, device_id_type=MESH)

    def send(src, dst, ss, rs, to):
        c = pltpu.make_async_remote_copy(
            src_ref=src, dst_ref=dst, send_sem=ss, recv_sem=rs, device_id=to, device_id_type=MESH
        )
        c.start()
        return c

    mine = pl.ds(pl.multiple_of(96 * n, 32), 96)
    loc = [
        pltpu.make_async_copy(tok_hbm, tok, loc_sem.at[0]),
        pltpu.make_async_copy(wo_hbm, wo.at[mine], loc_sem.at[1]),
    ]
    for m in range(3):
        for t in range(3):
            src = wp_hbm.at[:, pl.ds(pl.multiple_of(768 * m + 256 * t + 128 * core, 128), 128)]
            dst = wp.at[m, mine, pl.ds(128 * t, 128)]
            loc.append(pltpu.make_async_copy(src, dst, loc_sem.at[2 + 3 * m + t]))
    for c in loc[2:] + loc[:2]:
        c.start()
    perm[...] = jnp.where(iota((512, 512), 1) == tile_of_row(iota((512, 1), 0), core), 1.0, 0.0).astype(BF)
    for c in loc[2:]:
        c.wait()
    pl.semaphore_wait(barrier, len(partners))

    class Rows:
        def __init__(self, m, ss, rs):
            self.buf, self.ss, self.rs = wp.at[m], ss, rs
            self.sent = []

        def go(self, dx, other, first, count, to):
            j = ((1 - yl) if other else yl) * 4 + (x + dx) % 4
            ref = self.buf.at[pl.ds(pl.multiple_of(96 * j + first, 16), count)]
            k = len(self.sent)
            c = send(ref, ref, self.ss.at[k], self.rs.at[k], to)
            self.sent.append(c)
            return c

        def phase_a(self):
            self.a = [self.go(0, False, 0, 96, dev(dx=k)) for k in (1, 3, 2)]
            self.a += [self.go(0, False, 0, 48, dev(dy=1)), self.go(0, False, 48, 48, dev(dy=7))]

        def phase_b(self):
            self.a[0].wait_recv()
            self.b = [self.go(3, False, 0, 96, dev(dy=1))]
            self.a[1].wait_recv()
            self.b.append(self.go(1, False, 0, 96, dev(dy=7)))
            self.a[2].wait_recv()
            self.b += [self.go(2, False, 0, 48, dev(dy=1)), self.go(2, False, 48, 48, dev(dy=7))]

        def finish(self):
            for c in self.a[3:] + self.b:
                c.wait_recv()

    class Twin:
        def __init__(self):
            self.sent, self.passed = [], []
            self.left, self.right, self.full = pl.ds(0, 384), pl.ds(384, 384), pl.ds(0, 768)

        def at(self, dx, other, cols):
            j = ((1 - yl) if other else yl) * 4 + (x + dx) % 4
            return wo.at[pl.ds(pl.multiple_of(96 * j + 48 * core, 16), 48), cols]

        def go(self, ref, to):
            k = len(self.sent)
            c = send(ref, ref, os_.at[k], or_.at[k], to)
            self.sent.append(c)
            return c

        def twin(self, *refs):
            for ref in refs:
                self.passed.append(self.go(ref, dev(dc=1)))

        def phase_ax(self):
            self.a = [self.go(self.at(0, False, self.full), dev(dx=k)) for k in (1, 3, 2)]

        def phase_ay(self):
            self.a.append(self.go(self.at(0, False, self.left), dev(dy=1)))
            self.a.append(self.go(self.at(0, False, self.right), dev(dy=7)))

        def phase_b(self):
            a = self.a
            a[0].wait_recv()
            self.b = [self.go(self.at(3, False, self.full), dev(dy=1))]
            a[1].wait_recv()
            self.b.append(self.go(self.at(1, False, self.full), dev(dy=7)))
            a[2].wait_recv()
            self.b.append(self.go(self.at(2, False, self.left), dev(dy=1)))
            self.b.append(self.go(self.at(2, False, self.right), dev(dy=7)))
            self.twin(*[self.at(k, False, self.full) for k in (1, 2, 3)])
            a[3].wait_recv()
            a[4].wait_recv()
            self.twin(self.at(0, True, self.full))

        def phase_c(self):
            for c in self.b:
                c.wait_recv()
            self.twin(*[self.at(k, True, self.full) for k in (1, 2, 3)])

        def finish(self):
            for c in self.passed:
                c.wait_recv()

    gq, gk, gv = (Rows(m, ws.at[m], wr.at[m]) for m in range(3))
    outp = Twin()
    weights = (gk, gv, gq)
    for g in weights:
        g.phase_a()
    loc[0].wait()
    xo[...] = dot(perm[256:, :], tok[...]).astype(BF)
    tokens_sent = send(xo, xs.at[pl.ds(256, 256)], sc.at[0], rc.at[0], dev(dc=1))
    gk.phase_b()
    xs[:256, :] = dot(perm[:256, :], tok[...]).astype(BF)
    gv.phase_b()
    gq.phase_b()
    loc[1].wait()
    outp.phase_ax()
    outp.phase_ay()

    def project(m):
        qkv[:, 384 * m : 384 * m + 384] = dot(xs[...], wp[m]).astype(BF)

    low = iota((1, 128), 1) < 64
    row16 = iota((16, 128), 0)
    zeros8 = jnp.zeros((8, 128), F32)
    mine2 = pl.ds(pl.multiple_of(32 * n, 32), 32)

    def second(m, e, t):
        a = 256 * e + 32 * t
        c = 384 * m + 128 * t
        return jnp.where(low, qkv[a : a + 32, c : c + 128].astype(F32), qkv[a + 128 : a + 160, c : c + 128].astype(F32))

    def third(m):
        out = jnp.zeros((16, 128), F32)
        for e in range(2):
            for t in range(3):
                v = second(m, e, t)
                i = 4 * t + 2 * e
                if m > 0:
                    kv2[m - 1, e, mine2, 128 * t : 128 * t + 128] = v.astype(BF)
                u = jnp.concatenate([v[:8], zeros8], axis=0)
                if i:
                    u = pltpu.roll(u, i, 0)
                out = jnp.where((row16 >= i) & (row16 < i + 2), u, out)
        if m > 0:
            kv3[m - 1, x, yy] = out.astype(BF)
        else:
            q3[z] = out.astype(BF)

    tokens_sent.wait_recv()
    gk.finish()
    project(1)
    third(1)
    gv.finish()
    project(2)
    third(2)

    sent = [tokens_sent]
    k2 = k3 = 0

    def go3(src, dst, to):
        nonlocal k3
        c = send(src, dst, s3.at[k3], r3.at[k3], to)
        k3 += 1
        sent.append(c)
        return c

    def go2(ref, to):
        nonlocal k2
        c = send(ref, ref, s2.at[k2], r2.at[k2], to)
        k2 += 1
        sent.append(c)
        return c

    def at2(dx, other, e=None):
        j = ((1 - yl) if other else yl) * 4 + (x + dx) % 4
        return kv2.at[:, pl.ds(0, 2) if e is None else pl.ds(e, 1), pl.ds(pl.multiple_of(32 * j, 32), 32)]

    own3 = kv3.at[:, x, yy]
    a3 = [go3(own3, own3, dev(dy=k)) for k in (4, 3, 5, 2, 6, 1, 7)]
    pair = (w, (1 - yl) * 4 + x)
    u = [go2(at2(0, False), to) for to in (dev(dx=1), dev(dx=3))]
    gq.finish()
    project(0)
    third(0)
    sq = [go3(q3.at[z], q3.at[z], dev(dz=k)) for k in (4, 3, 5, 2, 6, 1, 7)]
    u.append(go2(at2(0, False), pair))

    first = {}

    def level1(e, t):
        o = []
        for lo in range(2):
            r = slice(256 * e + 128 * lo, 256 * e + 128 * lo + 128)
            q = jnp.where(low if lo == 0 else ~low, qkv[r, 128 * t : 128 * t + 128].astype(F32), 0.0).astype(BF)
            pk, tot, num = soft(q, qkv[r, 384 + 128 * t : 512 + 128 * t], qkv[r, 768 + 128 * t : 896 + 128 * t])
            o.append(num / tot)
            b = slice(32 * t, 32 * t + 32)
            first[e, t, lo] = pk[b], tot[b], num[b]
        att[e, :, 128 * t : 128 * t + 128] = jnp.where(low, o[0], o[1]).astype(BF)

    for c in a3:
        c.wait_recv()
    plane = kv3.at[:, x]
    b3 = [go3(plane, plane, dev(dx=k)) for k in (2, 1, 3)]
    u[0].wait_recv()
    v1 = go2(at2(3, False, 0), dev(dx=1))
    u[1].wait_recv()
    v2 = go2(at2(1, False, 1), dev(dx=3))
    outp.phase_b()
    level1(0, 0)
    level1(0, 1)
    u[2].wait_recv()
    g2 = [go2(at2(0, True), dev(dx=1)), go2(at2(0, True), dev(dx=3))]
    for c in b3 + sq:
        c.wait_recv()

    qa = q3[...].reshape(128, 128).astype(F32)
    qs = jnp.concatenate([jnp.where(low, qa, 0.0), jnp.where(low, 0.0, qa)], axis=0).astype(BF)
    same = (iota((256, 512), 0) % 16) // 4 == (iota((256, 512), 1) % 16) // 4
    pk, tot, num = soft(qs, kv3[0].reshape(512, 128), kv3[1].reshape(512, 128), same)
    num = jnp.where(low, num[:128], num[128:]).reshape(8, 16, 128)
    row, lane = iota((8, 16, 128), 1), iota((8, 16, 128), 2)

    def to_lanes(v):
        a, b = v[:128].reshape(8, 16, 1), v[128:].reshape(8, 16, 1)
        u = jnp.where(lane == row, a, jnp.where(lane == row + 64, b, 0.0))
        return jnp.sum(u, axis=1, keepdims=True)

    part_out[...] = jnp.where(row < 12, num, jnp.where(row == 12, to_lanes(pk), to_lanes(tot)))
    sp = [go3(part_out.at[(z + k) % 8], part_in.at[z], dev(dz=k)) for k in (4, 3, 5, 2, 6, 1, 7)]
    part_in[z] = part_out[z]
    v1.wait_recv()
    v2.wait_recv()
    g2.append(go2(at2(2, False), pair))
    level1(0, 2)
    for t in range(3):
        level1(1, t)
    outp.phase_c()

    for c in g2:
        c.wait_recv()
    both = {}
    for e in range(2):
        for t in range(3):
            v = second(0, e, t)
            q = jnp.concatenate([jnp.where(low, v, 0.0), jnp.where(low, 0.0, v)], axis=0).astype(BF)
            pk, tot, num = soft(q, kv2[0, e, :, 128 * t : 128 * t + 128], kv2[1, e, :, 128 * t : 128 * t + 128])
            for lo in range(2):
                b = slice(32 * lo, 32 * lo + 32)
                both[e, t, lo] = merge(first[e, t, lo], (pk[b], tot[b], num[b]))

    outp.finish()
    for g in weights + (outp,):
        sent += g.sent
    for c in sent:
        if not any(c is d for d in sp):
            c.wait_send()
    for c in sp:
        c.wait_recv()
    p = part_in[...]

    def from_lanes(v):
        a = jnp.sum(jnp.where(lane == row, v, 0.0), axis=-1, keepdims=True)
        b = jnp.sum(jnp.where(lane == row + 64, v, 0.0), axis=-1, keepdims=True)
        return jnp.where(lane < 64, a, b)

    pk, tot = from_lanes(p[:, 12:13]), from_lanes(p[:, 13:14])
    top = jnp.max(pk, axis=0)
    f = jnp.exp(pk - top[None])
    dist = (top, jnp.sum(tot * f, axis=0), jnp.sum(p * f, axis=0))

    use = iota((8, 128), 0) < 2

    def complete(e):
        for t in range(3):
            i = 4 * t + 2 * e
            d = [pltpu.roll(v, 16 - i, 0)[:8] if i else v[:8] for v in dist]
            d = (jnp.where(use, d[0], LOW), jnp.where(use, d[1], 0.0), jnp.where(use, d[2], 0.0))
            o = []
            for lo in range(2):
                pk, tot, num = both[e, t, lo]
                _, tot8, num8 = merge((pk[:8], tot[:8], num[:8]), d)
                o.append(jnp.concatenate([num8 / tot8, num[8:] / tot[8:]], axis=0))
            att[e, 32 * t : 32 * t + 32, 128 * t : 128 * t + 128] = jnp.where(low, o[0], o[1]).astype(BF)

    low384 = iota((1, 384), 1) % 128 < 64

    def output(e, packed):
        v = packed.astype(F32)
        rows = jnp.concatenate([jnp.where(low384, v, 0.0), jnp.where(low384, 0.0, v)], axis=0).astype(BF)
        at = [256 * t + 128 * ((core + e) % 2) for t in range(3)]
        wc = jnp.concatenate([wo[pl.ds(pl.multiple_of(a, 128), 128), :] for a in at], axis=0)
        y[256 * e : 256 * e + 256, :] = dot(rows, wc).astype(BF)

    complete(1)
    swap = send(att.at[1], got, sc.at[1], rc.at[1], dev(dc=1))
    complete(0)
    output(0, att[0])
    swap.wait_recv()
    output(1, got[...])
    for c in sp + [swap]:
        c.wait_send()


def in_order(y, out_ref):
    core = lax.axis_index("wide") % 2
    p = iota((256, 512), 0) + 256 * pl.program_id(0)
    back = jnp.where(p == tile_of_row(iota((1, 512), 1), core), 1.0, 0.0).astype(BF)
    out_ref[...] = dot(back, y[...]).astype(BF)


def shards(tokens, proj_weight, out_weight):
    hbm = pl.BlockSpec(memory_space=pl.ANY)
    dma = pltpu.SemaphoreType.DMA
    rows = pl.pallas_call(
        kernel,
        out_shape=pltpu.VMEM((512, 768), BF),
        in_specs=[hbm] * 3,
        out_specs=pl.BlockSpec(memory_space=pltpu.VMEM),
        scratch_shapes=[
            pltpu.VMEM((512, 768), BF),
            pltpu.VMEM((512, 512), BF),
            pltpu.VMEM((512, 768), BF),
            pltpu.VMEM((256, 768), BF),
            pltpu.VMEM((3, 768, 384), BF),
            pltpu.VMEM((768, 768), BF),
            pltpu.VMEM((512, 1152), BF),
            pltpu.VMEM((2, 2, 256, 384), BF),
            pltpu.VMEM((2, 4, 8, 16, 128), BF),
            pltpu.VMEM((8, 16, 128), BF),
            pltpu.VMEM((8, 16, 128), F32),
            pltpu.VMEM((8, 16, 128), F32),
            pltpu.VMEM((2, 128, 384), BF),
            pltpu.VMEM((128, 384), BF),
            dma((11,)),
            dma((3, 12)), dma((3, 12)), dma((16,)), dma((16,)),
            dma((8,)), dma((8,)), dma((24,)), dma((24,)), dma((2,)), dma((2,)),
        ],
        compiler_params=pltpu.CompilerParams(collective_id=0, has_side_effects=True, vmem_limit_bytes=56 << 20),
    )(tokens, proj_weight, out_weight)
    return pl.pallas_call(
        in_order,
        out_shape=jax.ShapeDtypeStruct((512, 768), BF),
        grid=(2,),
        in_specs=[pl.BlockSpec(memory_space=pltpu.VMEM)],
        out_specs=pl.BlockSpec((256, 768), lambda i: (i, 0)),
        compiler_params=pltpu.CompilerParams(vmem_limit_bytes=16 << 20),
    )(rows)


def solution(mesh):
    return jax.shard_map(
        shards,
        mesh=mesh,
        in_specs=(P(("wide", "narrow"), None), P("narrow", None), P("narrow", None)),
        out_specs=P(("wide", "narrow"), None),
        check_vma=False,
    )
```

```python
import jax
import jax.numpy as jnp
from jax import lax
from jax.experimental import pallas as pl
from jax.experimental.pallas import tpu as pltpu
from jax.sharding import PartitionSpec as P

MESH = pl.DeviceIdType.MESH
BF = jnp.bfloat16
F32 = jnp.float32
SCALE = 0.125
LOW = -1e30


def iota(shape, dim):
    return lax.broadcasted_iota(jnp.int32, shape, dim)


def tile_of_row(r, core):
    j = r % 32
    s = jnp.where(j == 1, 16, jnp.where((j >= 2) & (j <= 16), j - 1, j))
    return 16 * s + 4 * ((r // 32) % 4) + 2 * ((r // 256 + core) % 2) + (r // 128) % 2


def dot(a, b):
    return jnp.dot(a, b, preferred_element_type=F32)


def dot_t(a, b):
    return lax.dot_general(a, b, (((1,), (1,)), ((), ())), preferred_element_type=F32)


def soft(q, k, v, mask=None):
    s = dot_t(q, k) * SCALE
    if mask is not None:
        s = jnp.where(mask, s, LOW)
    peak = jnp.max(s, axis=-1, keepdims=True)
    w = jnp.exp(s - peak)
    return peak, jnp.sum(w, axis=-1, keepdims=True), dot(w.astype(BF), v)


def merge(a, b):
    top = jnp.maximum(a[0], b[0])
    ea, eb = jnp.exp(a[0] - top), jnp.exp(b[0] - top)
    return top, a[1] * ea + b[1] * eb, a[2] * ea + b[2] * eb


def kernel(
    tok_hbm, wp_hbm, wo_hbm, y,
    tok, perm, xs, xo, wp, wo, qkv, kv2, kv3, q3, part_out, part_in, att, got,
    loc_sem, ws, wr, os_, or_, s2, r2, s3, r3, sc, rc,
):
    w, n = lax.axis_index("wide"), lax.axis_index("narrow")
    x, yl, core, z, yh = n % 4, n // 4, w % 2, (w // 2) % 8, w // 16
    yy = 2 * yh + yl

    def dev(dx=0, dy=0, dz=0, dc=0):
        y_ = (yy + dy) % 8
        return ((y_ // 2) * 16 + ((z + dz) % 8) * 2 + (core + dc) % 2, (y_ % 2) * 4 + (x + dx) % 4)

    barrier = pltpu.get_barrier_semaphore()
    partners = (
        [dev(dx=k) for k in (1, 2, 3)] + [dev(dy=k) for k in range(1, 8)] + [dev(dz=k) for k in range(1, 8)] + [dev(dc=1)]
    )
    for p in partners:
        pl.semaphore_signal(barrier, inc=1, device_id=p, device_id_type=MESH)

    def send(src, dst, ss, rs, to):
        c = pltpu.make_async_remote_copy(
            src_ref=src, dst_ref=dst, send_sem=ss, recv_sem=rs, device_id=to, device_id_type=MESH
        )
        c.start()
        return c

    mine = pl.ds(pl.multiple_of(96 * n, 32), 96)
    loc = [
        pltpu.make_async_copy(tok_hbm, tok, loc_sem.at[0]),
        pltpu.make_async_copy(wo_hbm, wo.at[mine], loc_sem.at[1]),
    ]
    for m in range(3):
        for t in range(3):
            src = wp_hbm.at[:, pl.ds(pl.multiple_of(768 * m + 256 * t + 128 * core, 128), 128)]
            dst = wp.at[m, mine, pl.ds(128 * t, 128)]
            loc.append(pltpu.make_async_copy(src, dst, loc_sem.at[2 + 3 * m + t]))
    for c in loc[2:] + loc[:2]:
        c.start()
    perm[...] = jnp.where(iota((512, 512), 1) == tile_of_row(iota((512, 1), 0), core), 1.0, 0.0).astype(BF)
    for c in loc[2:]:
        c.wait()
    pl.semaphore_wait(barrier, len(partners))

    class Rows:
        def __init__(self, m, ss, rs):
            self.buf, self.ss, self.rs = wp.at[m], ss, rs
            self.sent = []

        def go(self, dx, other, first, count, to):
            j = ((1 - yl) if other else yl) * 4 + (x + dx) % 4
            ref = self.buf.at[pl.ds(pl.multiple_of(96 * j + first, 16), count)]
            k = len(self.sent)
            c = send(ref, ref, self.ss.at[k], self.rs.at[k], to)
            self.sent.append(c)
            return c

        def phase_a(self):
            self.a = [self.go(0, False, 0, 96, dev(dx=k)) for k in (1, 3, 2)]
            self.a += [self.go(0, False, 0, 48, dev(dy=1)), self.go(0, False, 48, 48, dev(dy=7))]

        def phase_b(self):
            self.a[0].wait_recv()
            self.b = [self.go(3, False, 0, 96, dev(dy=1))]
            self.a[1].wait_recv()
            self.b.append(self.go(1, False, 0, 96, dev(dy=7)))
            self.a[2].wait_recv()
            self.b += [self.go(2, False, 0, 48, dev(dy=1)), self.go(2, False, 48, 48, dev(dy=7))]

        def finish(self):
            for c in self.a[3:] + self.b:
                c.wait_recv()

    class Twin:
        def __init__(self):
            self.sent, self.passed = [], []
            self.left, self.right, self.full = pl.ds(0, 384), pl.ds(384, 384), pl.ds(0, 768)

        def at(self, dx, other, cols):
            j = ((1 - yl) if other else yl) * 4 + (x + dx) % 4
            return wo.at[pl.ds(pl.multiple_of(96 * j + 48 * core, 16), 48), cols]

        def go(self, ref, to):
            k = len(self.sent)
            c = send(ref, ref, os_.at[k], or_.at[k], to)
            self.sent.append(c)
            return c

        def twin(self, *refs):
            for ref in refs:
                self.passed.append(self.go(ref, dev(dc=1)))

        def phase_ax(self):
            self.a = [self.go(self.at(0, False, self.full), dev(dx=k)) for k in (1, 3, 2)]

        def phase_ay(self):
            self.a.append(self.go(self.at(0, False, self.left), dev(dy=1)))
            self.a.append(self.go(self.at(0, False, self.right), dev(dy=7)))

        def phase_b(self):
            a = self.a
            a[0].wait_recv()
            self.b = [self.go(self.at(3, False, self.full), dev(dy=1))]
            a[1].wait_recv()
            self.b.append(self.go(self.at(1, False, self.full), dev(dy=7)))
            a[2].wait_recv()
            self.b.append(self.go(self.at(2, False, self.left), dev(dy=1)))
            self.b.append(self.go(self.at(2, False, self.right), dev(dy=7)))
            self.twin(*[self.at(k, False, self.full) for k in (1, 2, 3)])
            a[3].wait_recv()
            a[4].wait_recv()
            self.twin(self.at(0, True, self.full))

        def phase_c(self):
            for c in self.b:
                c.wait_recv()
            self.twin(*[self.at(k, True, self.full) for k in (1, 2, 3)])

        def finish(self):
            for c in self.passed:
                c.wait_recv()

    gq, gk, gv = (Rows(m, ws.at[m], wr.at[m]) for m in range(3))
    outp = Twin()
    weights = (gk, gv, gq)
    for g in weights:
        g.phase_a()
    loc[0].wait()
    xo[...] = dot(perm[256:, :], tok[...]).astype(BF)
    tokens_sent = send(xo, xs.at[pl.ds(256, 256)], sc.at[0], rc.at[0], dev(dc=1))
    gk.phase_b()
    xs[:256, :] = dot(perm[:256, :], tok[...]).astype(BF)
    gv.phase_b()
    gq.phase_b()
    loc[1].wait()
    outp.phase_ax()
    outp.phase_ay()

    def project(m):
        qkv[:, 384 * m : 384 * m + 384] = dot(xs[...], wp[m]).astype(BF)

    low = iota((1, 128), 1) < 64
    row16 = iota((16, 128), 0)
    zeros8 = jnp.zeros((8, 128), F32)
    mine2 = pl.ds(pl.multiple_of(32 * n, 32), 32)

    def second(m, e, t):
        a = 256 * e + 32 * t
        c = 384 * m + 128 * t
        return jnp.where(low, qkv[a : a + 32, c : c + 128].astype(F32), qkv[a + 128 : a + 160, c : c + 128].astype(F32))

    def third(m):
        out = jnp.zeros((16, 128), F32)
        for e in range(2):
            for t in range(3):
                v = second(m, e, t)
                i = 4 * t + 2 * e
                if m > 0:
                    kv2[m - 1, e, mine2, 128 * t : 128 * t + 128] = v.astype(BF)
                u = jnp.concatenate([v[:8], zeros8], axis=0)
                if i:
                    u = pltpu.roll(u, i, 0)
                out = jnp.where((row16 >= i) & (row16 < i + 2), u, out)
        if m > 0:
            kv3[m - 1, x, yy] = out.astype(BF)
        else:
            q3[z] = out.astype(BF)

    tokens_sent.wait_recv()
    gk.finish()
    project(1)
    third(1)
    gv.finish()
    project(2)
    third(2)

    sent = [tokens_sent]
    k2 = k3 = 0

    def go3(src, dst, to):
        nonlocal k3
        c = send(src, dst, s3.at[k3], r3.at[k3], to)
        k3 += 1
        sent.append(c)
        return c

    def go2(ref, to):
        nonlocal k2
        c = send(ref, ref, s2.at[k2], r2.at[k2], to)
        k2 += 1
        sent.append(c)
        return c

    def at2(dx, other, e=None):
        j = ((1 - yl) if other else yl) * 4 + (x + dx) % 4
        return kv2.at[:, pl.ds(0, 2) if e is None else pl.ds(e, 1), pl.ds(pl.multiple_of(32 * j, 32), 32)]

    own3 = kv3.at[:, x, yy]
    a3 = [go3(own3, own3, dev(dy=k)) for k in (4, 3, 5, 2, 6, 1, 7)]
    pair = (w, (1 - yl) * 4 + x)
    u = [go2(at2(0, False), to) for to in (dev(dx=1), dev(dx=3))]
    gq.finish()
    project(0)
    third(0)
    sq = [go3(q3.at[z], q3.at[z], dev(dz=k)) for k in (4, 3, 5, 2, 6, 1, 7)]
    u.append(go2(at2(0, False), pair))

    first = {}

    def level1(e, t):
        o = []
        for lo in range(2):
            r = slice(256 * e + 128 * lo, 256 * e + 128 * lo + 128)
            q = jnp.where(low if lo == 0 else ~low, qkv[r, 128 * t : 128 * t + 128].astype(F32), 0.0).astype(BF)
            pk, tot, num = soft(q, qkv[r, 384 + 128 * t : 512 + 128 * t], qkv[r, 768 + 128 * t : 896 + 128 * t])
            o.append(num / tot)
            b = slice(32 * t, 32 * t + 32)
            first[e, t, lo] = pk[b], tot[b], num[b]
        att[e, :, 128 * t : 128 * t + 128] = jnp.where(low, o[0], o[1]).astype(BF)

    for c in a3:
        c.wait_recv()
    plane = kv3.at[:, x]
    b3 = [go3(plane, plane, dev(dx=k)) for k in (2, 1, 3)]
    u[0].wait_recv()
    v1 = go2(at2(3, False, 0), dev(dx=1))
    u[1].wait_recv()
    v2 = go2(at2(1, False, 1), dev(dx=3))
    outp.phase_b()
    level1(0, 0)
    level1(0, 1)
    u[2].wait_recv()
    g2 = [go2(at2(0, True), dev(dx=1)), go2(at2(0, True), dev(dx=3))]
    for c in b3 + sq:
        c.wait_recv()

    qa = q3[...].reshape(128, 128).astype(F32)
    qs = jnp.concatenate([jnp.where(low, qa, 0.0), jnp.where(low, 0.0, qa)], axis=0).astype(BF)
    same = (iota((256, 512), 0) % 16) // 4 == (iota((256, 512), 1) % 16) // 4
    pk, tot, num = soft(qs, kv3[0].reshape(512, 128), kv3[1].reshape(512, 128), same)
    num = jnp.where(low, num[:128], num[128:]).reshape(8, 16, 128)
    row, lane = iota((8, 16, 128), 1), iota((8, 16, 128), 2)

    def to_lanes(v):
        a, b = v[:128].reshape(8, 16, 1), v[128:].reshape(8, 16, 1)
        u = jnp.where(lane == row, a, jnp.where(lane == row + 64, b, 0.0))
        return jnp.sum(u, axis=1, keepdims=True)

    part_out[...] = jnp.where(row < 12, num, jnp.where(row == 12, to_lanes(pk), to_lanes(tot)))
    sp = [go3(part_out.at[(z + k) % 8], part_in.at[z], dev(dz=k)) for k in (4, 3, 5, 2, 6, 1, 7)]
    part_in[z] = part_out[z]
    v1.wait_recv()
    v2.wait_recv()
    g2.append(go2(at2(2, False), pair))
    level1(0, 2)
    for t in range(3):
        level1(1, t)
    outp.phase_c()

    for c in g2:
        c.wait_recv()
    both = {}
    for e in range(2):
        for t in range(3):
            v = second(0, e, t)
            q = jnp.concatenate([jnp.where(low, v, 0.0), jnp.where(low, 0.0, v)], axis=0).astype(BF)
            pk, tot, num = soft(q, kv2[0, e, :, 128 * t : 128 * t + 128], kv2[1, e, :, 128 * t : 128 * t + 128])
            for lo in range(2):
                b = slice(32 * lo, 32 * lo + 32)
                both[e, t, lo] = merge(first[e, t, lo], (pk[b], tot[b], num[b]))
            o = [both[e, t, lo][2] / both[e, t, lo][1] for lo in range(2)]
            att[e, 32 * t : 32 * t + 32, 128 * t : 128 * t + 128] = jnp.where(low, o[0], o[1]).astype(BF)

    outp.finish()
    for g in weights + (outp,):
        sent += g.sent
    for c in sent:
        if not any(c is d for d in sp):
            c.wait_send()
    for c in sp:
        c.wait_recv()
    p = part_in[...]

    def from_lanes(v):
        a = jnp.sum(jnp.where(lane == row, v, 0.0), axis=-1, keepdims=True)
        b = jnp.sum(jnp.where(lane == row + 64, v, 0.0), axis=-1, keepdims=True)
        return jnp.where(lane < 64, a, b)

    pk, tot = from_lanes(p[:, 12:13]), from_lanes(p[:, 13:14])
    top = jnp.max(pk, axis=0)
    f = jnp.exp(pk - top[None])
    dist = (top, jnp.sum(tot * f, axis=0), jnp.sum(p * f, axis=0))

    use = iota((8, 128), 0) < 2

    def complete(e):
        for t in range(3):
            i = 4 * t + 2 * e
            d = [pltpu.roll(v, 16 - i, 0)[:8] if i else v[:8] for v in dist]
            d = (jnp.where(use, d[0], LOW), jnp.where(use, d[1], 0.0), jnp.where(use, d[2], 0.0))
            o = []
            for lo in range(2):
                pk, tot, num = both[e, t, lo]
                _, tot8, num8 = merge((pk[:8], tot[:8], num[:8]), d)
                o.append(jnp.concatenate([num8 / tot8, num[8:16] / tot[8:16]], axis=0))
            att[e, 32 * t : 32 * t + 16, 128 * t : 128 * t + 128] = jnp.where(low, o[0], o[1]).astype(BF)

    low384 = iota((1, 384), 1) % 128 < 64

    def output(e, packed):
        v = packed.astype(F32)
        rows = jnp.concatenate([jnp.where(low384, v, 0.0), jnp.where(low384, 0.0, v)], axis=0).astype(BF)
        at = [256 * t + 128 * ((core + e) % 2) for t in range(3)]
        wc = jnp.concatenate([wo[pl.ds(pl.multiple_of(a, 128), 128), :] for a in at], axis=0)
        y[256 * e : 256 * e + 256, :] = dot(rows, wc).astype(BF)

    complete(1)
    swap = send(att.at[1], got, sc.at[1], rc.at[1], dev(dc=1))
    complete(0)
    output(0, att[0])
    swap.wait_recv()
    output(1, got[...])
    for c in sp + [swap]:
        c.wait_send()


def in_order(y, out_ref):
    core = lax.axis_index("wide") % 2
    p = iota((256, 512), 0) + 256 * pl.program_id(0)
    back = jnp.where(p == tile_of_row(iota((1, 512), 1), core), 1.0, 0.0).astype(BF)
    out_ref[...] = dot(back, y[...]).astype(BF)


def shards(tokens, proj_weight, out_weight):
    hbm = pl.BlockSpec(memory_space=pl.ANY)
    dma = pltpu.SemaphoreType.DMA
    rows = pl.pallas_call(
        kernel,
        out_shape=pltpu.VMEM((512, 768), BF),
        in_specs=[hbm] * 3,
        out_specs=pl.BlockSpec(memory_space=pltpu.VMEM),
        scratch_shapes=[
            pltpu.VMEM((512, 768), BF),
            pltpu.VMEM((512, 512), BF),
            pltpu.VMEM((512, 768), BF),
            pltpu.VMEM((256, 768), BF),
            pltpu.VMEM((3, 768, 384), BF),
            pltpu.VMEM((768, 768), BF),
            pltpu.VMEM((512, 1152), BF),
            pltpu.VMEM((2, 2, 256, 384), BF),
            pltpu.VMEM((2, 4, 8, 16, 128), BF),
            pltpu.VMEM((8, 16, 128), BF),
            pltpu.VMEM((8, 16, 128), F32),
            pltpu.VMEM((8, 16, 128), F32),
            pltpu.VMEM((2, 128, 384), BF),
            pltpu.VMEM((128, 384), BF),
            dma((11,)),
            dma((3, 12)), dma((3, 12)), dma((16,)), dma((16,)),
            dma((8,)), dma((8,)), dma((24,)), dma((24,)), dma((2,)), dma((2,)),
        ],
        compiler_params=pltpu.CompilerParams(collective_id=0, has_side_effects=True, vmem_limit_bytes=56 << 20),
    )(tokens, proj_weight, out_weight)
    return pl.pallas_call(
        in_order,
        out_shape=jax.ShapeDtypeStruct((512, 768), BF),
        grid=(2,),
        in_specs=[pl.BlockSpec(memory_space=pltpu.VMEM)],
        out_specs=pl.BlockSpec((256, 768), lambda i: (i, 0)),
        compiler_params=pltpu.CompilerParams(vmem_limit_bytes=16 << 20),
    )(rows)


def solution(mesh):
    return jax.shard_map(
        shards,
        mesh=mesh,
        in_specs=(P(("wide", "narrow"), None), P("narrow", None), P("narrow", None)),
        out_specs=P(("wide", "narrow"), None),
        check_vma=False,
    )
```
